32 devices in a mesh: tensor: 8 (over y, x, core), dp: 4 (over z).
Axes of the slice: x: 2, y: 2, z: 4, core: 2. Of those that a mesh axis runs over, the one named last changes fastest.
Arguments:
- cotangent: bfloat16 [1024, 8192], P('dp', 'tensor'), may hold values from -12 to 12
- down_weight: bfloat16 [28672, 8192], P('tensor', 'dp'), may hold values from -0.0625 to 0.0625
- gate_pre: bfloat16 [1024, 28672], P('dp', 'tensor'), may hold values from -6 to 6
- up_pre: bfloat16 [1024, 28672], P('dp', 'tensor'), may hold values from -6 to 6
Outputs:
- factor: bfloat16 [8, 2, 5, 4, 3211264], P('tensor', None, None, 'dp')
The draws below stay inside these ranges and needn't reach their ends.
All inputs are finite; a program needn't handle non-finite values.
Results may differ from the reference program's by a relative error of at most 0.0057.
Values may be sent and summed in bfloat16 or wider, within the bound.
No kernel may reach another device: no remote copies, remote signals or barrier semaphores. Data moves between devices by JAX's collectives and lax.ppermute only.
A program may use at most 256 MiB of HBM per device.

```python
import math
import jax
import jax.numpy as jnp
from jax import lax

D = 8192
FF = 28672
TOKENS = 1024
N_TENSOR = 8
N_DP = 4


def draw_cotangent(key, part):
    value_key, spread_key = jax.random.split(jax.random.fold_in(key, 11))
    values = jnp.clip(jax.random.normal(value_key, (TOKENS, D), jnp.float32), -4.0, 4.0)
    spread = jnp.exp(jax.random.uniform(spread_key, (TOKENS, 1), jnp.float32, 0.0, math.log(10.0)))
    return (0.3 * values * spread).astype(jnp.bfloat16)


def level_of(stream_key, dims, cuts, smallest, largest):
    loudness = 1.0
    for position, blocks in cuts:
        draws = jax.random.uniform(jax.random.fold_in(jax.random.fold_in(stream_key, 6), position), (blocks,), jnp.float32, smallest / len(cuts), largest / len(cuts))
        loudness = loudness * jnp.repeat(jnp.exp(draws), dims[position] // blocks).reshape((-1,) + (1,) * (len(dims) - 1 - position))
    return loudness


def centred(stream_key, dims, deviation, bound, cuts=(), kind=jnp.bfloat16):
    array = deviation * jax.random.normal(stream_key, dims, jnp.float32)
    if cuts:
        array = array * level_of(stream_key, dims, cuts, -0.22, 0.18)
    return jnp.clip(array, -bound, bound).astype(kind)


def setup_inputs(seed: int = 0) -> dict:
    splits = jax.random.split(jax.random.key(seed), 5)
    return {
        "cotangent": draw_cotangent(jax.random.fold_in(splits[4], 71), 0),
        "down_weight": centred(splits[1], (FF, D), D ** -0.5, 0.0625, ((0, 8), (1, 4))),
        "gate_pre": centred(splits[2], (TOKENS, FF), 1.5, 6.0, ((0, 4), (1, 8))),
        "up_pre": centred(splits[3], (TOKENS, FF), 1.0, 6.0, ((0, 4), (1, 8))),
    }


def reference(cotangent, down_weight, gate_pre, up_pre):
    block_count = N_TENSOR
    block_width = FF // block_count
    band_width = block_count // 2 + 1
    slice_width = block_width // N_DP
    hidden_cot = jnp.dot(cotangent, down_weight.T, preferred_element_type=jnp.float32)
    gate_value = gate_pre.astype(jnp.float32)
    up_value = up_pre.astype(jnp.float32)
    sigmoid_gate = jax.nn.sigmoid(gate_value)
    grad_gate = (hidden_cot * up_value * sigmoid_gate * (1.0 + gate_value * (1.0 - sigmoid_gate))).astype(jnp.bfloat16)
    grad_up = (hidden_cot * gate_value * sigmoid_gate).astype(jnp.bfloat16)
    blocks = jnp.stack([grad_gate, grad_up]).reshape(2, TOKENS, block_count, block_width)

    def row_block(block_row):
        own_rows = lax.dynamic_index_in_dim(blocks, block_row, 2, keepdims=False).astype(jnp.float32)
        partner_index = ((block_row - jnp.arange(band_width).astype(jnp.int32)) % block_count).astype(jnp.int32)
        partner_cols = jnp.take(blocks, partner_index, axis=2).astype(jnp.float32)
        product = jnp.einsum("ftr,ftkc->fkrc", own_rows, partner_cols)
        tiles = (product * (1.0 / TOKENS)).astype(jnp.bfloat16)
        tiles = tiles.reshape(2, band_width, block_width, N_DP, slice_width)
        tiles = jnp.transpose(tiles, (0, 1, 3, 2, 4))
        return tiles.reshape(2, band_width, N_DP, block_width * slice_width)

    return lax.map(row_block, jnp.arange(block_count).astype(jnp.int32))
```

```python
import functools
import jax
import jax.numpy as jnp
from jax import lax
from jax.experimental import pallas as pl
from jax.experimental.pallas import tpu as pltpu
from jax.sharding import PartitionSpec as P

CHUNKS = 2
LANES = 128
CONTRACT_LAST = (((1,), (1,)), ((), ()))


def factor_kernel(band, chunk_rows, chunk_total, scale, rows_ref, *refs):
    columns = refs[: band * chunk_total]
    out_ref, held, wide, sems = refs[-4:]
    slice_width = held.shape[2]
    lane_tiles = slice_width // LANES
    stride = 2 * lane_tiles
    step, k = pl.program_id(0), pl.program_id(1)

    def column_copy(source, slot, chunk):
        return pltpu.make_async_copy(
            source,
            held.at[slot, :, pl.ds(chunk * chunk_rows, chunk_rows)],
            sems.at[slot, chunk],
        )

    @pl.when((step == 0) & (k == 0))
    def _():
        for slot in range(band):
            for chunk in range(chunk_total):
                column_copy(columns[slot * chunk_total + chunk], slot, chunk).start()

    @pl.when(step == 0)
    def _():
        for chunk in range(chunk_total):
            column_copy(columns[chunk], k, chunk).wait()

    for f in range(2):
        rows = rows_ref[0, f]
        for first in range(0, lane_tiles, 2):
            count = min(2, lane_tiles - first)
            part = held[k, f, pl.ds(first * LANES, count * LANES), :]
            product = lax.dot_general(
                rows, part, CONTRACT_LAST, preferred_element_type=jnp.float32
            )
            product = product * scale
            for extra in range(count):
                wide[pl.ds((first + extra) * 2 + f, chunk_rows, stride=stride), :] = product[
                    :, extra * LANES : (extra + 1) * LANES
                ]
    out_ref[0] = wide[...].astype(out_ref.dtype)


def factor_rows(rows, columns, chunk, previous, slice_width, scale):
    slices, _, chunk_rows, tokens = rows.shape
    band = len(columns)
    chunk_total = len(columns[0])
    lane_tiles = slice_width // LANES
    height = chunk_rows * 2 * lane_tiles
    operands = [rows] + [piece for pieces in columns for piece in pieces]
    anywhere = pl.BlockSpec(memory_space=pl.ANY)
    in_specs = [pl.BlockSpec((1, 2, chunk_rows, tokens), lambda s, k: (s, 0, 0, 0))]
    in_specs += [anywhere] * (len(operands) - 1)
    aliases = {}
    if previous is not None:
        aliases = {len(operands): 0}
        operands.append(previous)
        in_specs.append(anywhere)
    return pl.pallas_call(
        functools.partial(factor_kernel, band, chunk_rows, chunk_total, scale),
        grid=(slices, band),
        in_specs=in_specs,
        out_specs=pl.BlockSpec((1, height, LANES), lambda s, k: (k, s * chunk_total + chunk, 0)),
        out_shape=jax.ShapeDtypeStruct((band, slices * chunk_total * height, LANES), rows.dtype),
        scratch_shapes=[
            pltpu.VMEM((band, 2, slice_width, tokens), rows.dtype),
            pltpu.VMEM((height, LANES), jnp.float32),
            pltpu.SemaphoreType.DMA((band, chunk_total)),
        ],
        input_output_aliases=aliases,
        compiler_params=pltpu.CompilerParams(
            dimension_semantics=("arbitrary", "arbitrary"), vmem_limit_bytes=52 * 2**20
        ),
        cost_estimate=pl.CostEstimate(
            flops=4 * slices * chunk_rows * tokens * band * slice_width,
            bytes_accessed=4 * slices * chunk_rows * (tokens + band * slice_width)
            + 4 * band * slice_width * tokens,
            transcendentals=0,
        ),
    )(*operands)


def per_device(cotangent, down_weight, gate_pre, up_pre):
    blocks = lax.axis_size("tensor")
    groups = lax.axis_size("dp")
    own_block = lax.axis_index("tensor")
    own_group = lax.axis_index("dp")
    per_group = blocks // groups
    local_tokens, block_width = gate_pre.shape
    slice_width = block_width // groups
    all_tokens = local_tokens * groups
    half_band = blocks // 2
    chunk_rows = slice_width // CHUNKS

    to_plane = [
        ((m * per_group + q) * groups + g, (g * per_group + q) * groups + m)
        for m in range(groups)
        for q in range(per_group)
        for g in range(groups)
    ]
    sent = lax.ppermute(cotangent.T, ("tensor", "dp"), to_plane)
    features = lax.all_gather(sent, "tensor", axis=0, tiled=True)
    features = features.reshape(groups, -1, local_tokens)
    features = features.transpose(1, 0, 2).reshape(-1, all_tokens)

    saved = jnp.stack([gate_pre, up_pre])

    def saved_slice(index):
        return lax.dynamic_slice_in_dim(saved, (index % groups) * slice_width, slice_width, 2)

    pieces = [saved_slice(own_group)]
    for shift in range(1, groups):
        ring = [(d, (d + shift) % groups) for d in range(groups)]
        pieces.append(lax.ppermute(saved_slice(own_group + shift), "dp", ring))
    pieces = jnp.stack(pieces)
    saved_all = jnp.concatenate(
        [
            lax.dynamic_index_in_dim(pieces, (own_group - h) % groups, 0, keepdims=False)
            for h in range(groups)
        ],
        axis=1,
    )
    saved_all = saved_all.transpose(0, 2, 1)

    weight = down_weight.reshape(groups, slice_width, -1)

    def reduced(chunk):
        part = weight[:, chunk * chunk_rows : (chunk + 1) * chunk_rows]
        partial = lax.dot_general(
            part.reshape(groups * chunk_rows, -1),
            features,
            (((1,), (0,)), ((), ())),
            preferred_element_type=jnp.float32,
        ).reshape(groups, chunk_rows, all_tokens)

        def slot(offset):
            return lax.dynamic_index_in_dim(
                partial, (own_group + offset) % groups, 0, keepdims=False
            )

        from_left = from_right = None
        for step in range(1, groups):
            right, left = slot(groups - step), slot(step)
            if step > 1:
                right = right + from_left.astype(jnp.float32)
                left = left + from_right.astype(jnp.float32)
            from_left = lax.ppermute(
                right.astype(jnp.bfloat16), "dp", [(d, d + 1) for d in range(step)]
            )
            from_right = lax.ppermute(
                left.astype(jnp.bfloat16),
                "dp",
                [(d, d - 1) for d in range(groups - step, groups)],
            )
        return slot(0) + from_left.astype(jnp.float32) + from_right.astype(jnp.float32)

    def gradients(chunk):
        hidden_cot = reduced(chunk)
        local = saved_all[:, chunk * chunk_rows : (chunk + 1) * chunk_rows].astype(jnp.float32)
        gate_value, up_value = local[0], local[1]
        sigmoid_gate = jax.nn.sigmoid(gate_value)
        grad_gate = hidden_cot * up_value * sigmoid_gate * (1.0 + gate_value * (1.0 - sigmoid_gate))
        grad_up = hidden_cot * gate_value * sigmoid_gate
        return jnp.stack([grad_gate.astype(jnp.bfloat16), grad_up.astype(jnp.bfloat16)])

    def partners(own):
        found = {0: own}
        for k in range(2, half_band + 1, 2):
            found[k] = lax.ppermute(
                own, "tensor", [(t, (t + k) % blocks) for t in range(blocks)]
            )
        swap = [(t, t ^ 1) for t in range(blocks)]
        odd = own_block % 2 == 1
        for k in range(1, half_band, 2):
            found[k] = lax.ppermute(jnp.where(odd, found[k + 1], found[k - 1]), "tensor", swap)
        return [found[k] for k in range(half_band + 1)]

    rows, columns = [], []
    for chunk in range(CHUNKS):
        own = gradients(chunk)
        rows.append(lax.all_gather(own, "dp", axis=0))
        columns.append(partners(own))
    columns = [[columns[c][k] for c in range(CHUNKS)] for k in range(half_band + 1)]
    inverse_count = 1.0 / all_tokens

    if slice_width % LANES == 0 and chunk_rows % 16 == 0:
        result = None
        for chunk in range(CHUNKS):
            result = factor_rows(rows[chunk], columns, chunk, result, slice_width, inverse_count)
        result = result.reshape(half_band + 1, -1, 2, LANES).transpose(2, 0, 1, 3)
    else:
        all_rows = jnp.concatenate(rows, axis=2)
        all_columns = jnp.stack([jnp.concatenate(pieces, axis=1) for pieces in columns])
        result = jnp.einsum(
            "sfrt,kfct->fksrc", all_rows, all_columns, preferred_element_type=jnp.float32
        )
        result = (result * inverse_count).astype(jnp.bfloat16)
    return result.reshape(1, 2, half_band + 1, 1, block_width * slice_width)


def solution(mesh):
    placed = (P("dp", "tensor"), P("tensor", "dp"), P("dp", "tensor"), P("dp", "tensor"))
    return jax.shard_map(
        per_device,
        mesh=mesh,
        in_specs=placed,
        out_specs=P("tensor", None, None, "dp", None),
        check_vma=False,
    )
```

```python
import functools
import jax
import jax.numpy as jnp
from jax import lax
from jax.experimental import pallas as pl
from jax.experimental.pallas import tpu as pltpu
from jax.sharding import PartitionSpec as P

CHUNKS = 2
LANES = 128
CONTRACT_LAST = (((1,), (1,)), ((), ()))


def factor_kernel(shape, candidates, scale, table_ref, *refs):
    band, chunk_total, chunk_rows = shape
    pieces = len(candidates)
    total = pieces * band
    row_refs = refs[: sum(candidates)]
    columns = refs[len(row_refs) : len(row_refs) + band * chunk_total]
    out_ref, held, rows_held, wide_even, wide_odd, column_sems, row_sems = refs[-7:]
    wides = (wide_even, wide_odd)
    slice_width = held.shape[2]
    lane_tiles = slice_width // LANES
    stride = 2 * lane_tiles
    step = pl.program_id(0)
    piece, k = step // band, step % band

    def column_copy(source, slot, chunk):
        return pltpu.make_async_copy(
            source,
            held.at[slot, :, pl.ds(chunk * chunk_rows, chunk_rows)],
            column_sems.at[slot, chunk],
        )

    def row_copy(source, slot):
        return pltpu.make_async_copy(source, rows_held.at[slot], row_sems.at[slot])

    def fetch(wanted):
        first = sum(candidates[:wanted])
        for choice in range(candidates[wanted]):

            @pl.when(table_ref[pieces + wanted] == choice)
            def _():
                row_copy(row_refs[first + choice], wanted % 2).start()

    @pl.when(step == 0)
    def _():
        fetch(0)
        for slot in range(band):
            for chunk in range(chunk_total):
                column_copy(columns[slot * chunk_total + chunk], slot, chunk).start()

    @pl.when((k == 0) & (step < total))
    def _():
        row_copy(row_refs[0], piece % 2).wait()

    for following in range(1, pieces):

        @pl.when(step == (following - 1) * band)
        def _():
            fetch(following)

    @pl.when(step < band)
    def _():
        for chunk in range(chunk_total):
            column_copy(columns[chunk], k, chunk).wait()

    def lay_out(wide):
        out_ref[0] = wide[...].astype(out_ref.dtype)

    def multiply(wide):
        for f in range(2):
            rows = rows_held[piece % 2, f]
            for first in range(0, lane_tiles, 2):
                count = min(2, lane_tiles - first)
                part = held[k, f, pl.ds(first * LANES, count * LANES), :]
                product = lax.dot_general(
                    rows, part, CONTRACT_LAST, preferred_element_type=jnp.float32
                )
                product = product * scale
                for extra in range(count):
                    start = (first + extra) * 2 + f
                    wide[pl.ds(start, chunk_rows, stride=stride), :] = product[
                        :, extra * LANES : (extra + 1) * LANES
                    ]

    for parity in range(2):

        @pl.when((step % 2 == parity) & (step < total))
        def _():
            multiply(wides[parity])
            lay_out(wides[1 - parity])

    @pl.when(step == total)
    def _():
        lay_out(wides[(total - 1) % 2])


def factor_rows(pieces, columns, previous, slices, slice_width, scale):
    _, chunk_rows, tokens = pieces[0][0][0].shape
    dtype = pieces[0][0][0].dtype
    band = len(columns)
    chunk_total = len(columns[0])
    lane_tiles = slice_width // LANES
    height = chunk_rows * 2 * lane_tiles
    count = len(pieces)
    table = jnp.stack(
        [jnp.int32(position) for _, _, position in pieces]
        + [jnp.int32(choice) for _, choice, _ in pieces]
    )
    operands = [array for arrays, _, _ in pieces for array in arrays]
    operands += [part for parts in columns for part in parts]
    aliases = {}
    if previous is not None:
        aliases = {1 + len(operands): 0}
        operands.append(previous)

    def placed(step, table_ref):
        done = jnp.maximum(step - 1, 0)
        return done % band, table_ref[done // band], 0

    return pl.pallas_call(
        functools.partial(
            factor_kernel,
            (band, chunk_total, chunk_rows),
            tuple(len(arrays) for arrays, _, _ in pieces),
            scale,
        ),
        grid_spec=pltpu.PrefetchScalarGridSpec(
            num_scalar_prefetch=1,
            grid=(count * band + 1,),
            in_specs=[pl.BlockSpec(memory_space=pl.ANY)] * len(operands),
            out_specs=pl.BlockSpec((1, height, LANES), placed),
            scratch_shapes=[
                pltpu.VMEM((band, 2, slice_width, tokens), dtype),
                pltpu.VMEM((2, 2, chunk_rows, tokens), dtype),
                pltpu.VMEM((height, LANES), jnp.float32),
                pltpu.VMEM((height, LANES), jnp.float32),
                pltpu.SemaphoreType.DMA((band, chunk_total)),
                pltpu.SemaphoreType.DMA((2,)),
            ],
        ),
        out_shape=jax.ShapeDtypeStruct((band, slices * chunk_total * height, LANES), dtype),
        input_output_aliases=aliases,
        compiler_params=pltpu.CompilerParams(
            dimension_semantics=("arbitrary",), vmem_limit_bytes=48 * 2**20
        ),
        cost_estimate=pl.CostEstimate(
            flops=4 * count * chunk_rows * tokens * band * slice_width,
            bytes_accessed=4 * count * chunk_rows * (tokens + band * slice_width)
            + 4 * band * slice_width * tokens,
            transcendentals=0,
        ),
    )(table, *operands)


def tie(*arrays):
    return lax.optimization_barrier(arrays)


def arrivals(groups, d):
    found = []
    for hops in range(1, groups):
        if d + hops < groups:
            found.append((hops, False))
        if d - hops >= 0:
            found.append((hops, True))
    return found


def per_device(cotangent, down_weight, gate_pre, up_pre):
    blocks = lax.axis_size("tensor")
    groups = lax.axis_size("dp")
    own_block = lax.axis_index("tensor")
    own_group = lax.axis_index("dp")
    per_group = blocks // groups
    local_tokens, block_width = gate_pre.shape
    local_features = cotangent.shape[1]
    slice_width = block_width // groups
    all_tokens = local_tokens * groups
    half_band = blocks // 2
    chunk_rows = slice_width // CHUNKS

    to_plane = [
        ((m * per_group + q) * groups + g, (q * groups + g) * groups + m)
        for m in range(groups)
        for q in range(per_group)
        for g in range(groups)
    ]
    sent = lax.ppermute(cotangent, ("tensor", "dp"), to_plane)
    sent, gate_pre, up_pre = tie(sent, gate_pre, up_pre)
    features = lax.all_gather(sent, "tensor", axis=0, tiled=True)

    saved = jnp.stack([gate_pre, up_pre])

    def saved_slice(index):
        return lax.dynamic_slice_in_dim(saved, (index % groups) * slice_width, slice_width, 2)

    pieces = [saved_slice(own_group)]
    for shift in range(1, groups):
        ring = [(d, (d + shift) % groups) for d in range(groups)]
        pieces.append(lax.ppermute(saved_slice(own_group + shift), "dp", ring))
    features, pieces[1], pieces[-1] = tie(features, pieces[1], pieces[-1])
    features = features.reshape(per_group, all_tokens, local_features)

    weight = down_weight.reshape(groups, slice_width, -1)

    def partial_products(chunk, features):
        part = weight[:, chunk * chunk_rows : (chunk + 1) * chunk_rows]
        part = part.reshape(groups * chunk_rows, per_group, local_features)
        return lax.dot_general(
            part,
            features,
            (((1, 2), (0, 2)), ((), ())),
            preferred_element_type=jnp.float32,
        ).reshape(groups, chunk_rows, all_tokens)

    def slot(partial, offset):
        return lax.dynamic_index_in_dim(partial, (own_group + offset) % groups, 0, keepdims=False)

    def reduce_step(partial, step, received):
        right, left = slot(partial, groups - step), slot(partial, step)
        if received is not None:
            right = right + received[0].astype(jnp.float32)
            left = left + received[1].astype(jnp.float32)
        return (
            lax.ppermute(right.astype(jnp.bfloat16), "dp", [(d, d + 1) for d in range(step)]),
            lax.ppermute(
                left.astype(jnp.bfloat16),
                "dp",
                [(d, d - 1) for d in range(groups - step, groups)],
            ),
        )

    def order_saved(pieces):
        pieces = jnp.stack(pieces)
        return jnp.concatenate(
            [
                lax.dynamic_index_in_dim(pieces, (own_group - h) % groups, 0, keepdims=False)
                for h in range(groups)
            ],
            axis=1,
        ).transpose(0, 2, 1)

    def gradients(partial, received, saved_all, chunk):
        hidden_cot = (
            slot(partial, 0) + received[0].astype(jnp.float32) + received[1].astype(jnp.float32)
        )
        local = saved_all[:, chunk * chunk_rows : (chunk + 1) * chunk_rows].astype(jnp.float32)
        gate_value, up_value = local[0], local[1]
        sigmoid_gate = jax.nn.sigmoid(gate_value)
        grad_gate = hidden_cot * up_value * sigmoid_gate * (1.0 + gate_value * (1.0 - sigmoid_gate))
        grad_up = hidden_cot * gate_value * sigmoid_gate
        return jnp.stack([grad_gate.astype(jnp.bfloat16), grad_up.astype(jnp.bfloat16)])

    def gather_step(step, left, right):
        return (
            lax.ppermute(left, "dp", [(d, d + 1) for d in range(step - 1, groups - 1)]),
            lax.ppermute(right, "dp", [(d, d - 1) for d in range(1, groups - step + 1)]),
        )

    shifts = list(range(half_band, 0, -2))
    turns = max(groups - 2, 1)

    def partner_step(step, found):
        if step <= turns:
            for k in shifts[step - 1 :: turns]:
                found[k] = lax.ppermute(
                    found[0], "tensor", [(t, (t + k) % blocks) for t in range(blocks)]
                )
        if step == groups - 1:
            swap = [(t, t ^ 1) for t in range(blocks)]
            odd = own_block % 2 == 1
            for k in range(1, half_band, 2):
                found[k] = lax.ppermute(jnp.where(odd, found[k + 1], found[k - 1]), "tensor", swap)

    partial = partial_products(0, features)
    received = reduce_step(partial, 1, None)
    received = tie(*received, *pieces)
    received, pieces = received[:2], received[2:]
    saved_all = order_saved(pieces)
    for step in range(2, groups):
        received = reduce_step(partial, step, received)
    rows, columns = [], []
    for chunk in range(CHUNKS):
        own = gradients(partial, received, saved_all, chunk)
        own, features = tie(own, features)
        later = chunk + 1 < CHUNKS
        if later:
            partial = partial_products(chunk + 1, features)
        found = {0: own}
        held = {}
        left = right = own
        received = None
        for step in range(1, groups):
            if later and step > 1:
                received = reduce_step(partial, step - 1, received)
            left, right = gather_step(step, left, right)
            partner_step(step, found)
            if later or step < groups - 1:
                keys = [k for k in found if k]
                moved = tie(left, right, *[found[k] for k in keys], *(received or ()))
                left, right = moved[:2]
                for place, k in enumerate(keys):
                    found[k] = moved[2 + place]
                if received is not None:
                    received = moved[-2:]
            held[step] = (right, left)
        if later:
            received = reduce_step(partial, groups - 1, received)
        rows.append((own, held))
        columns.append([found[k] for k in range(half_band + 1)])
    columns = [[columns[c][k] for c in range(CHUNKS)] for k in range(half_band + 1)]
    inverse_count = 1.0 / all_tokens

    if slice_width % LANES == 0 and chunk_rows % 16 == 0:
        order = [arrivals(groups, d) for d in range(groups)]

        def by_plane(values):
            return jnp.asarray(values, jnp.int32)[own_group]

        def row_piece(chunk, place):
            own, held = rows[chunk]
            if place == 0:
                return [own], 0, own_group * CHUNKS + chunk
            wanted = [order[d][place - 1] for d in range(groups)]
            kinds = sorted(set(wanted))
            origin = [d - hops if left else d + hops for d, (hops, left) in enumerate(wanted)]
            return (
                [held[hops][int(left)] for hops, left in kinds],
                by_plane([kinds.index(kind) for kind in wanted]),
                by_plane(origin) * CHUNKS + chunk,
            )

        pieces = [row_piece(chunk, place) for chunk in range(CHUNKS) for place in range(groups)]
        early = len(pieces) - groups // 2
        result = factor_rows(
            pieces[:early], columns, None, groups, slice_width, inverse_count
        )
        result = factor_rows(
            pieces[early:], columns, result, groups, slice_width, inverse_count
        )
        result = result.reshape(half_band + 1, -1, 2, LANES).transpose(2, 0, 1, 3)
    else:

        def in_order(own, held):
            turned = [own]
            for offset in range(1, groups):
                from_right = own_group + offset < groups
                turned.append(jnp.where(from_right, held[offset][0], held[groups - offset][1]))
            return jnp.roll(jnp.stack(turned), own_group, axis=0)

        all_rows = jnp.concatenate([in_order(*pair) for pair in rows], axis=2)
        all_columns = jnp.stack([jnp.concatenate(parts, axis=1) for parts in columns])
        result = jnp.einsum(
            "sfrt,kfct->fksrc", all_rows, all_columns, preferred_element_type=jnp.float32
        )
        result = (result * inverse_count).astype(jnp.bfloat16)
    return result.reshape(1, 2, half_band + 1, 1, block_width * slice_width)


def solution(mesh):
    placed = (P("dp", "tensor"), P("tensor", "dp"), P("dp", "tensor"), P("dp", "tensor"))
    return jax.shard_map(
        per_device,
        mesh=mesh,
        in_specs=placed,
        out_specs=P("tensor", None, None, "dp", None),
        check_vma=False,
    )
```

```python
import functools
import jax
import jax.numpy as jnp
from jax import lax
from jax.experimental import pallas as pl
from jax.experimental.pallas import tpu as pltpu
from jax.sharding import PartitionSpec as P

CHUNKS = 2
LANES = 128
CONTRACT_LAST = (((1,), (1,)), ((), ()))


def hidden_kernel(count, table_ref, weight_ref, features_ref, out_ref):
    groups, per_group, local_tokens, local_features = features_ref.shape
    for g in range(groups):
        place = table_ref[count + g]
        total = None
        for q in range(per_group):
            part = lax.dot_general(
                weight_ref[:, q * local_features : (q + 1) * local_features],
                features_ref[place, q],
                CONTRACT_LAST,
                preferred_element_type=jnp.float32,
            )
            total = part if total is None else total + part
        out_ref[0, :, g * local_tokens : (g + 1) * local_tokens] = total


def hidden_parts(weight, features, chunk, chunk_rows, offsets, own_group):
    groups, per_group, local_tokens, local_features = features.shape
    width = weight.shape[1]
    tokens = groups * local_tokens
    count = len(offsets)
    table = jnp.stack(
        [(own_group + offset) % groups * CHUNKS + chunk for offset in offsets]
        + [(own_group + g) % groups for g in range(groups)]
    ).astype(jnp.int32)
    return pl.pallas_call(
        functools.partial(hidden_kernel, count),
        grid_spec=pltpu.PrefetchScalarGridSpec(
            num_scalar_prefetch=1,
            grid=(count,),
            in_specs=[
                pl.BlockSpec((chunk_rows, width), lambda i, table_ref: (table_ref[i], 0)),
                pl.BlockSpec(features.shape, lambda i, table_ref: (0, 0, 0, 0)),
            ],
            out_specs=pl.BlockSpec((1, chunk_rows, tokens), lambda i, table_ref: (i, 0, 0)),
        ),
        out_shape=jax.ShapeDtypeStruct((count, chunk_rows, tokens), jnp.float32),
        compiler_params=pltpu.CompilerParams(
            dimension_semantics=("arbitrary",), vmem_limit_bytes=32 * 2**20
        ),
        cost_estimate=pl.CostEstimate(
            flops=2 * count * chunk_rows * tokens * width,
            bytes_accessed=count * chunk_rows * (2 * width + 4 * tokens) + 2 * tokens * width,
            transcendentals=0,
        ),
    )(table, weight, features)


def factor_kernel(shape, candidates, plan, scale, table_ref, *refs):
    partners, chunk_total, chunk_rows = shape
    total = len(plan)
    row_refs = refs[: sum(candidates)]
    columns = refs[len(row_refs) : len(row_refs) + partners * chunk_total]
    out_ref, held, rows_held, wide_even, wide_odd, column_sems, row_sems = refs[-7:]
    wides = (wide_even, wide_odd)
    slice_width = held.shape[2]
    lane_tiles = slice_width // LANES
    stride = 2 * lane_tiles
    step = pl.program_id(0)
    current = jnp.minimum(step, total - 1)
    slot, buffer = table_ref[2 * total + current], table_ref[3 * total + current]
    loads = [i for i in range(total) if i == 0 or plan[i][0] != plan[i - 1][0]]
    firsts = {}
    for i, (_, k) in enumerate(plan):
        firsts.setdefault(k, i)

    def column_copy(k, chunk):
        return pltpu.make_async_copy(
            columns[k * chunk_total + chunk],
            held.at[k, :, pl.ds(chunk * chunk_rows, chunk_rows)],
            column_sems.at[k, chunk],
        )

    def row_copy(source, place):
        return pltpu.make_async_copy(source, rows_held.at[place], row_sems.at[place])

    def fetch(load):
        piece = plan[loads[load]][0]
        first = sum(candidates[:piece])
        for choice in range(candidates[piece]):

            @pl.when(table_ref[4 * total + piece] == choice)
            def _():
                row_copy(row_refs[first + choice], load % 2).start()

    @pl.when(step == 0)
    def _():
        fetch(0)
        for k in sorted(firsts, key=firsts.get):
            for chunk in range(chunk_total):
                column_copy(k, chunk).start()

    for load, i in enumerate(loads):

        @pl.when(step == i)
        def _():
            row_copy(row_refs[0], load % 2).wait()
            if load + 1 < len(loads):
                fetch(load + 1)

    for k, i in firsts.items():

        @pl.when(step == i)
        def _():
            for chunk in range(chunk_total):
                column_copy(k, chunk).wait()

    def lay_out(wide):
        out_ref[0] = wide[...].astype(out_ref.dtype)

    def multiply(wide):
        for f in range(2):
            rows = rows_held[buffer, f]
            for first in range(0, lane_tiles, 2):
                count = min(2, lane_tiles - first)
                part = held[slot, f, pl.ds(first * LANES, count * LANES), :]
                product = lax.dot_general(
                    rows, part, CONTRACT_LAST, preferred_element_type=jnp.float32
                )
                product = product * scale
                for extra in range(count):
                    start = (first + extra) * 2 + f
                    wide[pl.ds(start, chunk_rows, stride=stride), :] = product[
                        :, extra * LANES : (extra + 1) * LANES
                    ]

    for parity in range(2):

        @pl.when((step % 2 == parity) & (step < total))
        def _():
            multiply(wides[parity])
            lay_out(wides[1 - parity])

    @pl.when(step == total)
    def _():
        lay_out(wides[(total - 1) % 2])


def factor_rows(pieces, columns, plan, previous, band, slices, scale):
    used = sorted(pieces)
    plan = [(used.index(piece), k) for piece, k in plan]
    pieces = [pieces[piece] for piece in used]
    keys = sorted({k for _, k in plan})
    _, chunk_rows, tokens = pieces[0][0][0].shape
    dtype = pieces[0][0][0].dtype
    chunk_total = len(columns[keys[0]])
    slice_width = chunk_total * chunk_rows
    height = chunk_rows * 2 * (slice_width // LANES)
    buffers, last = [], None
    for piece, _ in plan:
        if not buffers:
            buffers.append(0)
        else:
            buffers.append(buffers[-1] if piece == last else 1 - buffers[-1])
        last = piece
    table = jnp.stack(
        [jnp.int32(pieces[piece][2]) for piece, _ in plan]
        + [jnp.int32(k) for _, k in plan]
        + [jnp.int32(keys.index(k)) for _, k in plan]
        + [jnp.int32(buffer) for buffer in buffers]
        + [jnp.int32(choice) for _, choice, _ in pieces]
    )
    operands = [array for arrays, _, _ in pieces for array in arrays]
    operands += [part for k in keys for part in columns[k]]
    aliases = {}
    if previous is not None:
        aliases = {1 + len(operands): 0}
        operands.append(previous)
    total = len(plan)

    def placed(step, table_ref):
        done = jnp.maximum(step - 1, 0)
        return table_ref[total + done], table_ref[done], 0

    return pl.pallas_call(
        functools.partial(
            factor_kernel,
            (len(keys), chunk_total, chunk_rows),
            tuple(len(arrays) for arrays, _, _ in pieces),
            tuple((piece, keys.index(k)) for piece, k in plan),
            scale,
        ),
        grid_spec=pltpu.PrefetchScalarGridSpec(
            num_scalar_prefetch=1,
            grid=(total + 1,),
            in_specs=[pl.BlockSpec(memory_space=pl.ANY)] * len(operands),
            out_specs=pl.BlockSpec((1, height, LANES), placed),
            scratch_shapes=[
                pltpu.VMEM((len(keys), 2, slice_width, tokens), dtype),
                pltpu.VMEM((2, 2, chunk_rows, tokens), dtype),
                pltpu.VMEM((height, LANES), jnp.float32),
                pltpu.VMEM((height, LANES), jnp.float32),
                pltpu.SemaphoreType.DMA((len(keys), chunk_total)),
                pltpu.SemaphoreType.DMA((2,)),
            ],
        ),
        out_shape=jax.ShapeDtypeStruct((band, slices * chunk_total * height, LANES), dtype),
        input_output_aliases=aliases,
        compiler_params=pltpu.CompilerParams(
            dimension_semantics=("arbitrary",), vmem_limit_bytes=48 * 2**20
        ),
        cost_estimate=pl.CostEstimate(
            flops=4 * total * chunk_rows * tokens * slice_width,
            bytes_accessed=4 * total * chunk_rows * (tokens + slice_width)
            + 4 * len(keys) * slice_width * tokens,
            transcendentals=0,
        ),
    )(table, *operands)


def tie(*arrays):
    return lax.optimization_barrier(arrays)


def arrivals(groups, d):
    found = []
    for hops in range(1, groups):
        if d + hops < groups:
            found.append((hops, False))
        if d - hops >= 0:
            found.append((hops, True))
    return found


def per_device(cotangent, down_weight, gate_pre, up_pre):
    blocks = lax.axis_size("tensor")
    groups = lax.axis_size("dp")
    own_block = lax.axis_index("tensor")
    own_group = lax.axis_index("dp")
    per_group = blocks // groups
    local_tokens, block_width = gate_pre.shape
    local_features = cotangent.shape[1]
    slice_width = block_width // groups
    all_tokens = local_tokens * groups
    half_band = blocks // 2
    chunk_rows = slice_width // CHUNKS
    use_kernels = (
        slice_width % LANES == 0
        and chunk_rows % 16 == 0
        and local_features % LANES == 0
        and local_tokens % LANES == 0
    )

    to_plane = [
        ((m * per_group + q) * groups + g, ((m + g) % groups * per_group + q) * groups + m)
        for m in range(groups)
        for q in range(per_group)
        for g in range(groups)
    ]
    sent = lax.ppermute(cotangent, ("tensor", "dp"), to_plane)
    sent, gate_pre, up_pre = tie(sent, gate_pre, up_pre)
    features = lax.all_gather(sent, "tensor", axis=0, tiled=True)

    saved = jnp.stack([gate_pre, up_pre])

    def saved_slice(index):
        return lax.dynamic_slice_in_dim(saved, (index % groups) * slice_width, slice_width, 2)

    saved_pieces = [saved_slice(own_group)]
    for shift in range(1, groups):
        ring = [(d, (d + shift) % groups) for d in range(groups)]
        saved_pieces.append(lax.ppermute(saved_slice(own_group + shift), "dp", ring))
    features, *saved_pieces = tie(features, *saved_pieces)
    features = features.reshape(groups, per_group, local_tokens, local_features)

    def partial_products(chunk, offsets, features):
        if use_kernels:
            made = hidden_parts(down_weight, features, chunk, chunk_rows, offsets, own_group)
            return {offset: made[place] for place, offset in enumerate(offsets)}
        ordered = jnp.roll(features, -own_group, axis=0)
        made = {}
        for offset in offsets:
            first = (own_group + offset) % groups * slice_width + chunk * chunk_rows
            part = lax.dynamic_slice_in_dim(down_weight, first, chunk_rows, 0)
            made[offset] = jnp.einsum(
                "uqw,gqtw->ugt",
                part.reshape(chunk_rows, per_group, local_features),
                ordered,
                preferred_element_type=jnp.float32,
            ).reshape(chunk_rows, all_tokens)
        return made

    def reduce_step(partial, step, received):
        right, left = partial[groups - step], partial[step]
        if received is not None:
            right = right + received[0].astype(jnp.float32)
            left = left + received[1].astype(jnp.float32)
        return (
            lax.ppermute(right.astype(jnp.bfloat16), "dp", [(d, d + 1) for d in range(step)]),
            lax.ppermute(
                left.astype(jnp.bfloat16),
                "dp",
                [(d, d - 1) for d in range(groups - step, groups)],
            ),
        )

    def order_saved(pieces):
        pieces = jnp.stack(pieces)
        return jnp.concatenate(
            [
                lax.dynamic_index_in_dim(pieces, (own_group - h) % groups, 0, keepdims=False)
                for h in range(groups)
            ],
            axis=1,
        ).transpose(0, 2, 1)

    def gradients(partial, received, saved_all, chunk):
        hidden_cot = partial[0] + received[0].astype(jnp.float32) + received[1].astype(jnp.float32)
        local = saved_all[:, chunk * chunk_rows : (chunk + 1) * chunk_rows].astype(jnp.float32)
        gate_value, up_value = local[0], local[1]
        sigmoid_gate = jax.nn.sigmoid(gate_value)
        grad_gate = hidden_cot * up_value * sigmoid_gate * (1.0 + gate_value * (1.0 - sigmoid_gate))
        grad_up = hidden_cot * gate_value * sigmoid_gate
        return jnp.stack([grad_gate.astype(jnp.bfloat16), grad_up.astype(jnp.bfloat16)])

    def gather_step(step, left, right):
        return (
            lax.ppermute(left, "dp", [(d, d + 1) for d in range(step - 1, groups - 1)]),
            lax.ppermute(right, "dp", [(d, d - 1) for d in range(1, groups - step + 1)]),
        )

    shifts = list(range(2, half_band + 1, 2))
    turns = max(groups - 2, 1)
    share = -(-len(shifts) // turns)

    def partner_step(step, found):
        made = {}
        if step > 1:
            swap = [(t, t ^ 1) for t in range(blocks)]
            odd = own_block % 2 == 1
            for k in range(1, half_band, 2):
                if k not in found and k - 1 in found and k + 1 in found:
                    made[k] = lax.ppermute(
                        jnp.where(odd, found[k + 1], found[k - 1]), "tensor", swap
                    )
        for k in shifts[(step - 1) * share : step * share]:
            made[k] = lax.ppermute(
                found[0], "tensor", [(t, (t + k) % blocks) for t in range(blocks)]
            )
        return made

    band = half_band + 1
    inverse_count = 1.0 / all_tokens
    order = [arrivals(groups, d) for d in range(groups)]

    ready = {0: 0}
    for place, k in enumerate(shifts):
        ready[k] = place // share + 1
    for k in range(1, half_band, 2):
        ready[k] = max(ready[k - 1], ready[k + 1]) + 0.5
    calls = {}
    for k in sorted(ready, key=ready.get):
        for chunk in range(CHUNKS):
            for place in range(groups):
                came = 0
                if chunk == CHUNKS - 1 and place:
                    came = max(order[d][place - 1][0] for d in range(groups))
                calls.setdefault(max(ready[k], came), []).append(((chunk, place), k))

    def by_plane(values):
        return jnp.asarray(values, jnp.int32)[own_group]

    def row_piece(chunk, place):
        own, held = rows[chunk]
        if place == 0:
            return [own], 0, own_group * CHUNKS + chunk
        wanted = [order[d][place - 1] for d in range(groups)]
        kinds = sorted(set(wanted))
        origin = [d - hops if left else d + hops for d, (hops, left) in enumerate(wanted)]
        return (
            [held[hops][int(left)] for hops, left in kinds],
            by_plane([kinds.index(kind) for kind in wanted]),
            by_plane(origin) * CHUNKS + chunk,
        )

    def multiply(since, until, result):
        for time in sorted(calls):
            if since <= time < until:
                plan = calls[time]
                pieces = {piece: row_piece(*piece) for piece, _ in plan}
                keys = {k for _, k in plan}
                parts = {k: [columns[c][k] for c in range(CHUNKS)] for k in keys}
                result = factor_rows(pieces, parts, plan, result, band, groups, inverse_count)
        return result

    first_offsets = sorted({1, groups - 1})
    other_offsets = [offset for offset in range(groups) if offset not in first_offsets]
    partial = partial_products(0, first_offsets, features)
    received = reduce_step(partial, 1, None)
    partial.update(partial_products(0, other_offsets, features))
    received = tie(*received, *saved_pieces)
    received, saved_pieces = received[:2], received[2:]
    saved_all = order_saved(saved_pieces)
    for step in range(2, groups):
        received = tie(*reduce_step(partial, step, received))
    rows, columns, result = [], [], None
    for chunk in range(CHUNKS):
        own = gradients(partial, received, saved_all, chunk)
        own, features = tie(own, features)
        later = chunk + 1 < CHUNKS
        partial, received = {}, ()
        if later:
            partial = partial_products(chunk + 1, list(range(groups)), features)
        held, column, found = {}, {0: own}, {0: own}
        rows.append((own, held))
        columns.append(column)
        left = right = own
        for step in range(1, groups):
            if later and step > 1:
                received = reduce_step(partial, step - 1, received or None)
            left, right = gather_step(step, left, right)
            held[step] = (right, left)
            made = partner_step(step, found)
            column.update(made)
            found.update(made)
            if use_kernels and not later:
                result = multiply(step - 1.5, step - 0.5, result)
            if step < groups - 1 or later:
                keys, offsets = list(found), list(partial) if step == 1 else []
                moved = tie(
                    left, right, *received, *[found[k] for k in keys], *[partial[o] for o in offsets]
                )
                left, right = moved[:2]
                moved = moved[2:]
                received, moved = moved[: len(received)], moved[len(received) :]
                found = dict(zip(keys, moved))
                partial.update(zip(offsets, moved[len(keys) :]))
                if result is not None:
                    result, left, right = tie(result, left, right)
        if later:
            received = reduce_step(partial, groups - 1, received)

    if use_kernels:
        result = multiply(groups - 1.5, groups, result)
        result = result.reshape(band, -1, 2, LANES).transpose(2, 0, 1, 3)
    else:

        def in_order(own, held):
            turned = [own]
            for offset in range(1, groups):
                from_right = own_group + offset < groups
                turned.append(jnp.where(from_right, held[offset][0], held[groups - offset][1]))
            return jnp.roll(jnp.stack(turned), own_group, axis=0)

        all_rows = jnp.concatenate([in_order(*pair) for pair in rows], axis=2)
        all_columns = jnp.stack([jnp.concatenate([columns[c][k] for c in range(CHUNKS)], axis=1) for k in range(band)])
        result = jnp.einsum(
            "sfrt,kfct->fksrc", all_rows, all_columns, preferred_element_type=jnp.float32
        )
        result = (result * inverse_count).astype(jnp.bfloat16)
    return result.reshape(1, 2, band, 1, block_width * slice_width)


def solution(mesh):
    placed = (P("dp", "tensor"), P("tensor", "dp"), P("dp", "tensor"), P("dp", "tensor"))
    return jax.shard_map(
        per_device,
        mesh=mesh,
        in_specs=placed,
        out_specs=P("tensor", None, None, "dp", None),
        check_vma=False,
    )
```

```python
import functools
import jax
import jax.numpy as jnp
import numpy as np
from jax import lax
from jax.experimental import pallas as pl
from jax.experimental.pallas import tpu as pltpu
from jax.sharding import PartitionSpec as P

CHUNKS = 2
LANES = 128
CONTRACT_LAST = (((1,), (1,)), ((), ()))


def hidden_kernel(base, table_ref, weight_ref, features_ref, out_ref):
    groups, per_group, local_tokens, local_features = features_ref.shape
    for g in range(groups):
        place = table_ref[base + g]
        total = None
        for q in range(per_group):
            part = lax.dot_general(
                weight_ref[:, q * local_features : (q + 1) * local_features],
                features_ref[place, q],
                CONTRACT_LAST,
                preferred_element_type=jnp.float32,
            )
            total = part if total is None else total + part
        out_ref[0, :, g * local_tokens : (g + 1) * local_tokens] = total


def hidden_parts(weight, features, chunk_rows, table, base, count):
    groups, per_group, local_tokens, local_features = features.shape
    width = weight.shape[1]
    tokens = groups * local_tokens
    return pl.pallas_call(
        functools.partial(hidden_kernel, base + count),
        grid_spec=pltpu.PrefetchScalarGridSpec(
            num_scalar_prefetch=1,
            grid=(count,),
            in_specs=[
                pl.BlockSpec((chunk_rows, width), lambda i, table_ref: (table_ref[base + i], 0)),
                pl.BlockSpec(features.shape, lambda i, table_ref: (0, 0, 0, 0)),
            ],
            out_specs=pl.BlockSpec((1, chunk_rows, tokens), lambda i, table_ref: (i, 0, 0)),
        ),
        out_shape=jax.ShapeDtypeStruct((count, chunk_rows, tokens), jnp.float32),
        compiler_params=pltpu.CompilerParams(
            dimension_semantics=("arbitrary",), vmem_limit_bytes=56 * 2**20
        ),
        cost_estimate=pl.CostEstimate(
            flops=2 * count * chunk_rows * tokens * width,
            bytes_accessed=count * chunk_rows * (2 * width + 4 * tokens) + 2 * tokens * width,
            transcendentals=0,
        ),
    )(table, weight, features)


def factor_kernel(shape, candidates, plan, base, scale, table_ref, *refs):
    partners, chunk_total, chunk_rows = shape
    total = len(plan)
    row_refs = refs[: sum(candidates)]
    columns = refs[len(row_refs) : len(row_refs) + partners * chunk_total]
    out_ref, held, rows_held, wide_even, wide_odd, column_sems, row_sems = refs[-7:]
    wides = (wide_even, wide_odd)
    slice_width = held.shape[2]
    lane_tiles = slice_width // LANES
    stride = 2 * lane_tiles
    step = pl.program_id(0)
    current = jnp.minimum(step, total - 1)
    slot, buffer = table_ref[base + 2 * total + current], table_ref[base + 3 * total + current]
    loads = [i for i in range(total) if i == 0 or plan[i][0] != plan[i - 1][0]]
    firsts = {}
    for i, (_, k) in enumerate(plan):
        firsts.setdefault(k, i)

    def column_copy(k, chunk):
        return pltpu.make_async_copy(
            columns[k * chunk_total + chunk],
            held.at[k, :, pl.ds(chunk * chunk_rows, chunk_rows)],
            column_sems.at[k, chunk],
        )

    def row_copy(source, place):
        return pltpu.make_async_copy(source, rows_held.at[place], row_sems.at[place])

    def fetch(load):
        piece = plan[loads[load]][0]
        first = sum(candidates[:piece])
        for choice in range(candidates[piece]):

            @pl.when(table_ref[base + 4 * total + piece] == choice)
            def _():
                row_copy(row_refs[first + choice], load % 2).start()

    @pl.when(step == 0)
    def _():
        fetch(0)
        for k in sorted(firsts, key=firsts.get):
            for chunk in range(chunk_total):
                column_copy(k, chunk).start()

    for load, i in enumerate(loads):

        @pl.when(step == i)
        def _():
            row_copy(row_refs[0], load % 2).wait()
            if load + 1 < len(loads):
                fetch(load + 1)

    for k, i in firsts.items():

        @pl.when(step == i)
        def _():
            for chunk in range(chunk_total):
                column_copy(k, chunk).wait()

    def lay_out(wide):
        out_ref[0] = wide[...].astype(out_ref.dtype)

    def multiply(wide):
        for f in range(2):
            rows = rows_held[buffer, f]
            for first in range(0, lane_tiles, 2):
                count = min(2, lane_tiles - first)
                part = held[slot, f, pl.ds(first * LANES, count * LANES), :]
                product = lax.dot_general(
                    rows, part, CONTRACT_LAST, preferred_element_type=jnp.float32
                )
                product = product * scale
                for extra in range(count):
                    start = (first + extra) * 2 + f
                    wide[pl.ds(start, chunk_rows, stride=stride), :] = product[
                        :, extra * LANES : (extra + 1) * LANES
                    ]

    for parity in range(2):

        @pl.when((step % 2 == parity) & (step < total))
        def _():
            multiply(wides[parity])
            lay_out(wides[1 - parity])

    @pl.when(step == total)
    def _():
        lay_out(wides[(total - 1) % 2])


def factor_table(plan, used, keys, positions, choices):
    buffers = [0]
    for last, now in zip(plan, plan[1:]):
        buffers.append(buffers[-1] if last[0] == now[0] else 1 - buffers[-1])
    return (
        [positions[piece] for piece, _ in plan]
        + [k for _, k in plan]
        + [keys.index(k) for _, k in plan]
        + buffers
        + [choices[piece] for piece in used]
    )


def factor_rows(pieces, columns, plan, table, base, previous, band, slices, scale):
    used, keys = sorted(pieces), sorted(columns)
    plan = [(used.index(piece), k) for piece, k in plan]
    pieces = [pieces[piece] for piece in used]
    _, chunk_rows, tokens = pieces[0][0].shape
    dtype = pieces[0][0].dtype
    chunk_total = len(columns[keys[0]])
    slice_width = chunk_total * chunk_rows
    height = chunk_rows * 2 * (slice_width // LANES)
    operands = [array for arrays in pieces for array in arrays]
    operands += [part for k in keys for part in columns[k]]
    aliases = {}
    if previous is not None:
        aliases = {1 + len(operands): 0}
        operands.append(previous)
    total = len(plan)

    def placed(step, table_ref):
        done = jnp.maximum(step - 1, 0)
        return table_ref[base + total + done], table_ref[base + done], 0

    return pl.pallas_call(
        functools.partial(
            factor_kernel,
            (len(keys), chunk_total, chunk_rows),
            tuple(len(arrays) for arrays in pieces),
            tuple((piece, keys.index(k)) for piece, k in plan),
            base,
            scale,
        ),
        grid_spec=pltpu.PrefetchScalarGridSpec(
            num_scalar_prefetch=1,
            grid=(total + 1,),
            in_specs=[pl.BlockSpec(memory_space=pl.ANY)] * len(operands),
            out_specs=pl.BlockSpec((1, height, LANES), placed),
            scratch_shapes=[
                pltpu.VMEM((len(keys), 2, slice_width, tokens), dtype),
                pltpu.VMEM((2, 2, chunk_rows, tokens), dtype),
                pltpu.VMEM((height, LANES), jnp.float32),
                pltpu.VMEM((height, LANES), jnp.float32),
                pltpu.SemaphoreType.DMA((len(keys), chunk_total)),
                pltpu.SemaphoreType.DMA((2,)),
            ],
        ),
        out_shape=jax.ShapeDtypeStruct((band, slices * chunk_total * height, LANES), dtype),
        input_output_aliases=aliases,
        compiler_params=pltpu.CompilerParams(
            dimension_semantics=("arbitrary",), vmem_limit_bytes=48 * 2**20
        ),
        cost_estimate=pl.CostEstimate(
            flops=4 * total * chunk_rows * tokens * slice_width,
            bytes_accessed=4 * total * chunk_rows * (tokens + slice_width)
            + 4 * len(keys) * slice_width * tokens,
            transcendentals=0,
        ),
    )(table, *operands)


def tie(*arrays):
    return lax.optimization_barrier(arrays)


def arrivals(groups, d):
    found = []
    for hops in range(1, groups):
        if d + hops < groups:
            found.append((hops, False))
        if d - hops >= 0:
            found.append((hops, True))
    return found


def per_device(cotangent, down_weight, gate_pre, up_pre):
    blocks = lax.axis_size("tensor")
    groups = lax.axis_size("dp")
    own_block = lax.axis_index("tensor")
    own_group = lax.axis_index("dp")
    per_group = blocks // groups
    local_tokens, block_width = gate_pre.shape
    local_features = cotangent.shape[1]
    slice_width = block_width // groups
    all_tokens = local_tokens * groups
    half_band = blocks // 2
    chunk_rows = slice_width // CHUNKS
    use_kernels = (
        slice_width % LANES == 0
        and chunk_rows % 16 == 0
        and local_features % LANES == 0
        and local_tokens % LANES == 0
    )

    to_plane = [
        ((m * per_group + q) * groups + g, ((m + g) % groups * per_group + q) * groups + m)
        for m in range(groups)
        for q in range(per_group)
        for g in range(groups)
    ]
    sent = lax.ppermute(cotangent, ("tensor", "dp"), to_plane)
    saved = jnp.stack([gate_pre.T, up_pre.T])
    sent, saved = tie(sent, saved)
    features = lax.all_gather(sent, "tensor", axis=0, tiled=True)

    def saved_pieces(chunk, saved):
        def part(index):
            first = (index % groups) * slice_width + chunk * chunk_rows
            return lax.dynamic_slice_in_dim(saved, first, chunk_rows, 1)

        pieces = [part(own_group)]
        for shift in range(1, groups):
            ring = [(d, (d + shift) % groups) for d in range(groups)]
            pieces.append(lax.ppermute(part(own_group + shift), "dp", ring))
        return pieces

    def order_saved(pieces):
        pieces = jnp.stack(pieces)
        return jnp.concatenate(
            [
                lax.dynamic_index_in_dim(pieces, (own_group - h) % groups, 0, keepdims=False)
                for h in range(groups)
            ],
            axis=2,
        )

    first_saved = saved_pieces(0, saved)
    features, saved, *first_saved = tie(features, saved, *first_saved)
    features = features.reshape(groups, per_group, local_tokens, local_features)

    def partial_products(chunk, offsets, features):
        if use_kernels:
            base = bases["hidden", chunk, offsets]
            return hidden_parts(down_weight, features, chunk_rows, table, base, len(offsets))
        ordered = jnp.roll(features, -own_group, axis=0)
        made = []
        for offset in offsets:
            first = (own_group + offset) % groups * slice_width + chunk * chunk_rows
            part = lax.dynamic_slice_in_dim(down_weight, first, chunk_rows, 0)
            made.append(
                jnp.einsum(
                    "uqw,gqtw->ugt",
                    part.reshape(chunk_rows, per_group, local_features),
                    ordered,
                    preferred_element_type=jnp.float32,
                ).reshape(chunk_rows, all_tokens)
            )
        return jnp.stack(made)

    def reduce_step(partial, step, received):
        right, left = partial(groups - step), partial(step)
        if received is not None:
            right = right + received[0].astype(jnp.float32)
            left = left + received[1].astype(jnp.float32)
        return (
            lax.ppermute(right.astype(jnp.bfloat16), "dp", [(d, d + 1) for d in range(step)]),
            lax.ppermute(
                left.astype(jnp.bfloat16),
                "dp",
                [(d, d - 1) for d in range(groups - step, groups)],
            ),
        )

    def gradients(partial, received, saved):
        hidden_cot = partial(0) + received[0].astype(jnp.float32) + received[1].astype(jnp.float32)
        local = saved.astype(jnp.float32)
        gate_value, up_value = local[0], local[1]
        sigmoid_gate = jax.nn.sigmoid(gate_value)
        grad_gate = hidden_cot * up_value * sigmoid_gate * (1.0 + gate_value * (1.0 - sigmoid_gate))
        grad_up = hidden_cot * gate_value * sigmoid_gate
        return jnp.stack([grad_gate.astype(jnp.bfloat16), grad_up.astype(jnp.bfloat16)])

    def gather_step(step, left, right):
        return (
            lax.ppermute(left, "dp", [(d, d + 1) for d in range(step - 1, groups - 1)]),
            lax.ppermute(right, "dp", [(d, d - 1) for d in range(1, groups - step + 1)]),
        )

    shifts = list(range(2, half_band + 1, 2))
    turns = max(groups - 2, 1)
    share = -(-len(shifts) // turns)

    def partner_step(step, found):
        made = {}
        if step > 1:
            swap = [(t, t ^ 1) for t in range(blocks)]
            odd = own_block % 2 == 1
            for k in range(1, half_band, 2):
                if k not in found and k - 1 in found and k + 1 in found:
                    made[k] = lax.ppermute(
                        jnp.where(odd, found[k + 1], found[k - 1]), "tensor", swap
                    )
        for k in shifts[(step - 1) * share : step * share]:
            made[k] = lax.ppermute(
                found[0], "tensor", [(t, (t + k) % blocks) for t in range(blocks)]
            )
        return made

    band = half_band + 1
    inverse_count = 1.0 / all_tokens
    order = [arrivals(groups, d) for d in range(groups)]

    ready = {0: 0}
    for place, k in enumerate(shifts):
        ready[k] = place // share + 1
    for k in range(1, half_band, 2):
        ready[k] = max(ready[k - 1], ready[k + 1]) + 1
    calls = {}
    for k in sorted(ready, key=ready.get):
        for chunk in range(CHUNKS):
            for place in range(groups):
                came = 0
                if chunk == CHUNKS - 1 and place:
                    came = max(order[d][place - 1][0] for d in range(groups))
                calls.setdefault(max(ready[k], came), []).append(((chunk, place), k))

    def row_arrays(chunk, place):
        own, held = rows[chunk]
        if place == 0:
            return [own]
        kinds = sorted({order[d][place - 1] for d in range(groups)})
        return [held[hops][int(left)] for hops, left in kinds]

    def row_entry(d, chunk, place):
        if place == 0:
            return d * CHUNKS + chunk, 0
        kinds = sorted({order[e][place - 1] for e in range(groups)})
        hops, left = order[d][place - 1]
        return (d - hops if left else d + hops) * CHUNKS + chunk, kinds.index((hops, left))

    first_offsets = tuple(sorted({1, groups - 1}))
    other_offsets = tuple(o for o in range(groups) if o not in first_offsets)
    all_offsets = tuple(range(groups))
    hidden_calls = [(0, first_offsets), (0, other_offsets)]
    hidden_calls += [(chunk, all_offsets) for chunk in range(1, CHUNKS)]
    bases, lines = {}, [[] for _ in range(groups)]
    for chunk, offsets in hidden_calls:
        bases["hidden", chunk, offsets] = len(lines[0])
        for d in range(groups):
            lines[d] += [(d + offset) % groups * CHUNKS + chunk for offset in offsets]
            lines[d] += [(d + g) % groups for g in range(groups)]
    for time, plan in calls.items():
        bases["factor", time] = len(lines[0])
        used = sorted({piece for piece, _ in plan})
        keys = sorted({k for _, k in plan})
        for d in range(groups):
            entries = [row_entry(d, *piece) for piece in used]
            lines[d] += factor_table(
                [(used.index(piece), k) for piece, k in plan],
                list(range(len(used))),
                keys,
                [position for position, _ in entries],
                [choice for _, choice in entries],
            )
    table = lax.dynamic_index_in_dim(
        jnp.asarray(np.array(lines, np.int32)), own_group, 0, keepdims=False
    )

    def multiply(time, result):
        if time not in calls:
            return result
        plan = calls[time]
        pieces = {piece: row_arrays(*piece) for piece, _ in plan}
        parts = {k: [columns[c][k] for c in range(CHUNKS)] for _, k in plan}
        base = bases["factor", time]
        return factor_rows(
            pieces, parts, plan, table, base, result, band, groups, inverse_count
        )

    def lookup(*made):
        return lambda offset: next(
            array[offsets.index(offset)] for offsets, array in made if offset in offsets
        )

    first_parts = partial_products(0, first_offsets, features)
    other_parts = partial_products(0, other_offsets, features)
    partial = lookup((first_offsets, first_parts), (other_offsets, other_parts))
    later_saved = [saved_pieces(chunk, saved) for chunk in range(1, CHUNKS)]
    received = None
    for step in range(1, groups):
        received = tie(*reduce_step(partial, step, received))
        if step == groups - 2:
            moved = tie(*received, *[piece for pieces in later_saved for piece in pieces])
            received, moved = moved[:2], moved[2:]
            later_saved = [
                list(moved[c * groups : (c + 1) * groups]) for c in range(CHUNKS - 1)
            ]
    all_saved = [order_saved(pieces) for pieces in [first_saved, *later_saved]]
    rows, columns, result = [], [], None
    for chunk in range(CHUNKS):
        own = gradients(partial, received, all_saved[chunk])
        own, features = tie(own, features)
        later = chunk + 1 < CHUNKS
        received = ()
        if later:
            parts = partial_products(chunk + 1, all_offsets, features)
        held, column, found = {}, {0: own}, {0: own}
        rows.append((own, held))
        columns.append(column)
        left = right = own
        for step in range(1, groups):
            if later and step > 1:
                received = reduce_step(partial, step - 1, received or None)
            left, right = gather_step(step, left, right)
            held[step] = (right, left)
            made = partner_step(step, found)
            column.update(made)
            found.update(made)
            if use_kernels and not later:
                result = multiply(step - 1, result)
            if step < groups - 1 or later:
                keys = list(found)
                new_parts = [parts] if later and step == 1 else []
                moved = tie(left, right, *received, *[found[k] for k in keys], *new_parts)
                left, right = moved[:2]
                moved = moved[2:]
                received, moved = moved[: len(received)], moved[len(received) :]
                found = dict(zip(keys, moved))
                if new_parts:
                    partial = lookup((all_offsets, moved[-1]))
                if result is not None:
                    result, left, right = tie(result, left, right)
        column.update(partner_step(groups, found))
        if later:
            received = reduce_step(partial, groups - 1, received)

    if use_kernels:
        result = multiply(groups - 1, result)
        result = result.reshape(band, -1, 2, LANES).transpose(2, 0, 1, 3)
    else:

        def in_order(own, held):
            turned = [own]
            for offset in range(1, groups):
                from_right = own_group + offset < groups
                turned.append(jnp.where(from_right, held[offset][0], held[groups - offset][1]))
            return jnp.roll(jnp.stack(turned), own_group, axis=0)

        all_rows = jnp.concatenate([in_order(*pair) for pair in rows], axis=2)
        all_columns = jnp.stack([jnp.concatenate([columns[c][k] for c in range(CHUNKS)], axis=1) for k in range(band)])
        result = jnp.einsum(
            "sfrt,kfct->fksrc", all_rows, all_columns, preferred_element_type=jnp.float32
        )
        result = (result * inverse_count).astype(jnp.bfloat16)
    return result.reshape(1, 2, band, 1, block_width * slice_width)


def solution(mesh):
    placed = (P("dp", "tensor"), P("tensor", "dp"), P("dp", "tensor"), P("dp", "tensor"))
    return jax.shard_map(
        per_device,
        mesh=mesh,
        in_specs=placed,
        out_specs=P("tensor", None, None, "dp", None),
        check_vma=False,
    )
```

```python
import functools
import jax
import jax.numpy as jnp
import numpy as np
from jax import lax
from jax.experimental import pallas as pl
from jax.experimental.pallas import tpu as pltpu
from jax.sharding import PartitionSpec as P

CHUNKS = 1
LAST_PARTS = 2
LANES = 128
CONTRACT_LAST = (((1,), (1,)), ((), ()))


def hidden_kernel(base, table_ref, weight_ref, features_ref, out_ref):
    groups, per_group, local_tokens, local_features = features_ref.shape
    for g in range(groups):
        place = table_ref[base + g]
        total = None
        for q in range(per_group):
            part = lax.dot_general(
                weight_ref[:, q * local_features : (q + 1) * local_features],
                features_ref[place, q],
                CONTRACT_LAST,
                preferred_element_type=jnp.float32,
            )
            total = part if total is None else total + part
        out_ref[0, :, g * local_tokens : (g + 1) * local_tokens] = total


def hidden_parts(weight, features, chunk_rows, table, base, count):
    groups, per_group, local_tokens, local_features = features.shape
    width = weight.shape[1]
    tokens = groups * local_tokens
    return pl.pallas_call(
        functools.partial(hidden_kernel, base + count),
        grid_spec=pltpu.PrefetchScalarGridSpec(
            num_scalar_prefetch=1,
            grid=(count,),
            in_specs=[
                pl.BlockSpec((chunk_rows, width), lambda i, table_ref: (table_ref[base + i], 0)),
                pl.BlockSpec(features.shape, lambda i, table_ref: (0, 0, 0, 0)),
            ],
            out_specs=pl.BlockSpec((1, chunk_rows, tokens), lambda i, table_ref: (i, 0, 0)),
        ),
        out_shape=jax.ShapeDtypeStruct((count, chunk_rows, tokens), jnp.float32),
        compiler_params=pltpu.CompilerParams(
            dimension_semantics=("arbitrary",), vmem_limit_bytes=56 * 2**20
        ),
        cost_estimate=pl.CostEstimate(
            flops=2 * count * chunk_rows * tokens * width,
            bytes_accessed=count * chunk_rows * (2 * width + 4 * tokens) + 2 * tokens * width,
            transcendentals=0,
        ),
    )(table, weight, features)


def factor_kernel(shape, candidates, plan, base, scale, table_ref, *refs):
    partners, chunk_total, chunk_rows, row_count = shape
    total = len(plan)
    row_refs = refs[: sum(candidates)]
    columns = refs[len(row_refs) : len(row_refs) + partners * chunk_total]
    out_ref, held, rows_held, wide_even, wide_odd, column_sems, row_sems = refs[-7:]
    wides = (wide_even, wide_odd)
    slice_width = held.shape[2]
    lane_tiles = slice_width // LANES
    stride = 2 * lane_tiles
    step = pl.program_id(0)
    current = jnp.minimum(step, total - 1)
    slot, buffer = table_ref[base + 2 * total + current], table_ref[base + 3 * total + current]
    loads = [i for i in range(total) if i == 0 or plan[i][0] != plan[i - 1][0]]
    firsts = {}
    for i, (_, k) in enumerate(plan):
        firsts.setdefault(k, i)

    def column_copy(k, chunk):
        return pltpu.make_async_copy(
            columns[k * chunk_total + chunk],
            held.at[k, :, pl.ds(chunk * chunk_rows, chunk_rows)],
            column_sems.at[k, chunk],
        )

    def row_copy(source, place):
        return pltpu.make_async_copy(source, rows_held.at[place], row_sems.at[place])

    def fetch(load):
        piece = plan[loads[load]][0]
        first = sum(candidates[:piece])
        for choice in range(candidates[piece]):

            @pl.when(table_ref[base + 4 * total + piece] == choice)
            def _():
                row_copy(row_refs[first + choice], load % 2).start()

    @pl.when(step == 0)
    def _():
        fetch(0)
        for k in sorted(firsts, key=firsts.get):
            for chunk in range(chunk_total):
                column_copy(k, chunk).start()

    for load, i in enumerate(loads):

        @pl.when(step == i)
        def _():
            row_copy(row_refs[0], load % 2).wait()
            if load + 1 < len(loads):
                fetch(load + 1)

    for k, i in firsts.items():

        @pl.when(step == i)
        def _():
            for chunk in range(chunk_total):
                column_copy(k, chunk).wait()

    def lay_out(wide):
        out_ref[0] = wide[...].astype(out_ref.dtype)

    def multiply(wide):
        for f in range(2):
            rows = rows_held[buffer, f]
            for first in range(0, lane_tiles, 2):
                count = min(2, lane_tiles - first)
                part = held[slot, f, pl.ds(first * LANES, count * LANES), :]
                product = lax.dot_general(
                    rows, part, CONTRACT_LAST, preferred_element_type=jnp.float32
                )
                product = product * scale
                for extra in range(count):
                    start = (first + extra) * 2 + f
                    wide[pl.ds(start, row_count, stride=stride), :] = product[
                        :, extra * LANES : (extra + 1) * LANES
                    ]

    for parity in range(2):

        @pl.when((step % 2 == parity) & (step < total))
        def _():
            multiply(wides[parity])
            lay_out(wides[1 - parity])

    @pl.when(step == total)
    def _():
        lay_out(wides[(total - 1) % 2])


def factor_table(plan, used, keys, positions, choices):
    buffers = [0]
    for last, now in zip(plan, plan[1:]):
        buffers.append(buffers[-1] if last[0] == now[0] else 1 - buffers[-1])
    return (
        [positions[piece] for piece, _ in plan]
        + [k for _, k in plan]
        + [keys.index(k) for _, k in plan]
        + buffers
        + [choices[piece] for piece in used]
    )


def factor_rows(pieces, columns, plan, table, base, previous, band, slices, scale):
    used, keys = sorted(pieces), sorted(columns)
    plan = [(used.index(piece), k) for piece, k in plan]
    pieces = [pieces[piece] for piece in used]
    _, row_count, tokens = pieces[0][0].shape
    dtype = pieces[0][0].dtype
    chunk_total = len(columns[keys[0]])
    chunk_rows = columns[keys[0]][0].shape[1]
    slice_width = chunk_total * chunk_rows
    lane_tiles = slice_width // LANES
    height = row_count * 2 * lane_tiles
    operands = [array for arrays in pieces for array in arrays]
    operands += [part for k in keys for part in columns[k]]
    aliases = {}
    if previous is not None:
        aliases = {1 + len(operands): 0}
        operands.append(previous)
    total = len(plan)

    def placed(step, table_ref):
        done = jnp.maximum(step - 1, 0)
        return table_ref[base + total + done], table_ref[base + done], 0

    return pl.pallas_call(
        functools.partial(
            factor_kernel,
            (len(keys), chunk_total, chunk_rows, row_count),
            tuple(len(arrays) for arrays in pieces),
            tuple((piece, keys.index(k)) for piece, k in plan),
            base,
            scale,
        ),
        grid_spec=pltpu.PrefetchScalarGridSpec(
            num_scalar_prefetch=1,
            grid=(total + 1,),
            in_specs=[pl.BlockSpec(memory_space=pl.ANY)] * len(operands),
            out_specs=pl.BlockSpec((1, height, LANES), placed),
            scratch_shapes=[
                pltpu.VMEM((len(keys), 2, slice_width, tokens), dtype),
                pltpu.VMEM((2, 2, row_count, tokens), dtype),
                pltpu.VMEM((height, LANES), jnp.float32),
                pltpu.VMEM((height, LANES), jnp.float32),
                pltpu.SemaphoreType.DMA((len(keys), chunk_total)),
                pltpu.SemaphoreType.DMA((2,)),
            ],
        ),
        out_shape=jax.ShapeDtypeStruct(
            (band, slices * slice_width * 2 * lane_tiles, LANES), dtype
        ),
        input_output_aliases=aliases,
        compiler_params=pltpu.CompilerParams(
            dimension_semantics=("arbitrary",), vmem_limit_bytes=56 * 2**20
        ),
        cost_estimate=pl.CostEstimate(
            flops=4 * total * row_count * tokens * slice_width,
            bytes_accessed=4 * total * row_count * (tokens + slice_width)
            + 4 * len(keys) * slice_width * tokens,
            transcendentals=0,
        ),
    )(table, *operands)


def tie(*arrays):
    return lax.optimization_barrier(arrays)


def arrivals(groups, d):
    found = []
    for hops in range(1, groups):
        if d + hops < groups:
            found.append((hops, False))
        if d - hops >= 0:
            found.append((hops, True))
    return found


def per_device(cotangent, down_weight, gate_pre, up_pre):
    blocks = lax.axis_size("tensor")
    groups = lax.axis_size("dp")
    own_block = lax.axis_index("tensor")
    own_group = lax.axis_index("dp")
    per_group = blocks // groups
    local_tokens, block_width = gate_pre.shape
    local_features = cotangent.shape[1]
    slice_width = block_width // groups
    all_tokens = local_tokens * groups
    half_band = blocks // 2
    chunk_rows = slice_width // CHUNKS
    use_kernels = (
        slice_width % LANES == 0
        and chunk_rows % (16 * LAST_PARTS) == 0
        and local_features % LANES == 0
        and local_tokens % LANES == 0
    )

    to_plane = [
        ((m * per_group + q) * groups + g, ((m + g) % groups * per_group + q) * groups + m)
        for m in range(groups)
        for q in range(per_group)
        for g in range(groups)
    ]
    sent = lax.ppermute(cotangent, ("tensor", "dp"), to_plane)
    saved = jnp.stack([gate_pre.T, up_pre.T])
    sent, saved = tie(sent, saved)
    features = lax.all_gather(sent, "tensor", axis=0, tiled=True)

    def saved_pieces(chunk, saved):
        def part(index):
            first = (index % groups) * slice_width + chunk * chunk_rows
            return lax.dynamic_slice_in_dim(saved, first, chunk_rows, 1)

        pieces = [part(own_group)]
        for shift in range(1, groups):
            ring = [(d, (d + shift) % groups) for d in range(groups)]
            pieces.append(lax.ppermute(part(own_group + shift), "dp", ring))
        return pieces

    def order_saved(pieces):
        pieces = jnp.stack(pieces)
        return jnp.concatenate(
            [
                lax.dynamic_index_in_dim(pieces, (own_group - h) % groups, 0, keepdims=False)
                for h in range(groups)
            ],
            axis=2,
        )

    first_saved = saved_pieces(0, saved)
    features, first_saved[1], first_saved[-1] = tie(features, first_saved[1], first_saved[-1])
    features = features.reshape(groups, per_group, local_tokens, local_features)

    def partial_products(chunk, offsets, features):
        if use_kernels:
            base = bases["hidden", chunk, offsets]
            return hidden_parts(down_weight, features, chunk_rows, table, base, len(offsets))
        ordered = jnp.roll(features, -own_group, axis=0)
        made = []
        for offset in offsets:
            first = (own_group + offset) % groups * slice_width + chunk * chunk_rows
            part = lax.dynamic_slice_in_dim(down_weight, first, chunk_rows, 0)
            made.append(
                jnp.einsum(
                    "uqw,gqtw->ugt",
                    part.reshape(chunk_rows, per_group, local_features),
                    ordered,
                    preferred_element_type=jnp.float32,
                ).reshape(chunk_rows, all_tokens)
            )
        return jnp.stack(made)

    def reduce_step(partial, step, received):
        right, left = partial(groups - step), partial(step)
        if received is not None:
            right = right + received[0].astype(jnp.float32)
            left = left + received[1].astype(jnp.float32)
        return (
            lax.ppermute(right.astype(jnp.bfloat16), "dp", [(d, d + 1) for d in range(step)]),
            lax.ppermute(
                left.astype(jnp.bfloat16),
                "dp",
                [(d, d - 1) for d in range(groups - step, groups)],
            ),
        )

    def gradients(partial, received, saved):
        hidden_cot = partial(0) + received[0].astype(jnp.float32) + received[1].astype(jnp.float32)
        local = saved.astype(jnp.float32)
        gate_value, up_value = local[0], local[1]
        sigmoid_gate = jax.nn.sigmoid(gate_value)
        grad_gate = hidden_cot * up_value * sigmoid_gate * (1.0 + gate_value * (1.0 - sigmoid_gate))
        grad_up = hidden_cot * gate_value * sigmoid_gate
        return jnp.stack([grad_gate.astype(jnp.bfloat16), grad_up.astype(jnp.bfloat16)])

    def gather_step(step, left, right):
        return (
            lax.ppermute(left, "dp", [(d, d + 1) for d in range(step - 1, groups - 1)]),
            lax.ppermute(right, "dp", [(d, d - 1) for d in range(1, groups - step + 1)]),
        )

    shifts = list(range(2, half_band + 1, 2))
    turns = max(groups - 2, 1)
    share = -(-len(shifts) // turns)

    def partner_step(step, found):
        made = {}
        if step > 1:
            swap = [(t, t ^ 1) for t in range(blocks)]
            odd = own_block % 2 == 1
            for k in range(1, half_band, 2):
                if k not in found and k - 1 in found and k + 1 in found:
                    made[k] = lax.ppermute(
                        jnp.where(odd, found[k + 1], found[k - 1]), "tensor", swap
                    )
        for k in shifts[(step - 1) * share : step * share]:
            made[k] = lax.ppermute(
                found[0], "tensor", [(t, (t + k) % blocks) for t in range(blocks)]
            )
        return made

    band = half_band + 1
    inverse_count = 1.0 / all_tokens
    order = [arrivals(groups, d) for d in range(groups)]

    ready = {0: 0}
    for place, k in enumerate(shifts):
        ready[k] = place // share + 1
    for k in range(1, half_band, 2):
        ready[k] = max(ready[k - 1], ready[k + 1]) + 1
        if ready[k] == groups - 1:
            ready[k] -= 0.5
    calls = {}
    for k in sorted(ready, key=ready.get):
        for chunk in range(CHUNKS):
            for place in range(groups):
                came = 0
                if chunk == CHUNKS - 1 and place:
                    came = max(order[d][place - 1][0] for d in range(groups))
                if came == groups - 1:
                    for part in range(LAST_PARTS):
                        time = came + part / LAST_PARTS
                        calls.setdefault(time, []).append(((chunk, place, part), k))
                else:
                    calls.setdefault(max(ready[k], came), []).append(((chunk, place, None), k))

    part_rows = chunk_rows // LAST_PARTS

    def row_arrays(chunk, place, part):
        own, held = rows[chunk]
        if place == 0:
            return [own]
        kinds = sorted({order[d][place - 1] for d in range(groups)})
        arrays = [held[hops][int(left)] for hops, left in kinds]
        if part is None:
            return arrays
        return [
            parts[part] if hops == groups - 1 else piece_of(parts, part)
            for (hops, _), parts in zip(kinds, arrays)
        ]

    def piece_of(array, part):
        return array[:, part * part_rows : (part + 1) * part_rows]

    def row_entry(d, chunk, place, part):
        hops, left, choice = 0, False, 0
        if place:
            kinds = sorted({order[e][place - 1] for e in range(groups)})
            hops, left = order[d][place - 1]
            choice = kinds.index((hops, left))
        position = (d - hops if left else d + hops) * CHUNKS + chunk
        if part is not None:
            position = position * LAST_PARTS + part
        return position, choice

    first_offsets = tuple(sorted({1, groups - 1}))
    other_offsets = tuple(o for o in range(groups) if o not in first_offsets)
    all_offsets = tuple(range(groups))
    hidden_calls = [(0, first_offsets), (0, other_offsets)]
    hidden_calls += [(chunk, all_offsets) for chunk in range(1, CHUNKS)]
    bases, lines = {}, [[] for _ in range(groups)]
    for chunk, offsets in hidden_calls:
        bases["hidden", chunk, offsets] = len(lines[0])
        for d in range(groups):
            lines[d] += [(d + offset) % groups * CHUNKS + chunk for offset in offsets]
            lines[d] += [(d + g) % groups for g in range(groups)]
    for time, plan in calls.items():
        bases["factor", time] = len(lines[0])
        used = sorted({piece for piece, _ in plan})
        keys = sorted({k for _, k in plan})
        for d in range(groups):
            entries = [row_entry(d, *piece) for piece in used]
            lines[d] += factor_table(
                [(used.index(piece), k) for piece, k in plan],
                list(range(len(used))),
                keys,
                [position for position, _ in entries],
                [choice for _, choice in entries],
            )
    table = lax.dynamic_index_in_dim(
        jnp.asarray(np.array(lines, np.int32)), own_group, 0, keepdims=False
    )

    def multiply(time, result):
        if time not in calls:
            return result
        plan = calls[time]
        pieces = {piece: row_arrays(*piece) for piece, _ in plan}
        parts = {k: [columns[c][k] for c in range(CHUNKS)] for _, k in plan}
        base = bases["factor", time]
        return factor_rows(
            pieces, parts, plan, table, base, result, band, groups, inverse_count
        )

    def lookup(*made):
        return lambda offset: next(
            array[offsets.index(offset)] for offsets, array in made if offset in offsets
        )

    first_parts = partial_products(0, first_offsets, features)
    other_parts = partial_products(0, other_offsets, features)
    partial = lookup((first_offsets, first_parts), (other_offsets, other_parts))
    later_saved = [saved_pieces(chunk, saved) for chunk in range(1, CHUNKS)]
    received = None
    for step in range(1, groups):
        received = tie(*reduce_step(partial, step, received))
        if step == 1:
            moved = tie(*received, *first_saved)
            received, first_saved = moved[:2], list(moved[2:])
        if step == groups - 2 and later_saved:
            moved = tie(*received, *[piece for pieces in later_saved for piece in pieces])
            received, moved = moved[:2], moved[2:]
            later_saved = [
                list(moved[c * groups : (c + 1) * groups]) for c in range(CHUNKS - 1)
            ]
    all_saved = [order_saved(pieces) for pieces in [first_saved, *later_saved]]
    rows, columns, result = [], [], None
    for chunk in range(CHUNKS):
        own = gradients(partial, received, all_saved[chunk])
        own, features = tie(own, features)
        later = chunk + 1 < CHUNKS
        received = ()
        if later:
            parts = partial_products(chunk + 1, all_offsets, features)
        held, column, found = {}, {0: own}, {0: own}
        rows.append((own, held))
        columns.append(column)
        left = right = own
        for step in range(1, groups):
            if later and step > 1:
                received = reduce_step(partial, step - 1, received or None)
            made = partner_step(step, found)
            if step < groups - 1 or later or not use_kernels:
                left, right = gather_step(step, left, right)
                held[step] = (right, left)
            else:
                lefts, rights, sent_on = [], [], ()
                for part in range(LAST_PARTS):
                    ends = (piece_of(left, part), piece_of(right, part))
                    if sent_on:
                        ends = tie(*ends, *sent_on)[:2]
                    sent_on = gather_step(step, *ends)
                    lefts.append(sent_on[0])
                    rights.append(sent_on[1])
                held[step] = (rights, lefts)
            column.update(made)
            found.update(made)
            if use_kernels and not later:
                result = multiply(step - 1, result)
                result = multiply(step - 0.5, result)
            if step < groups - 1 or later:
                keys = list(found)
                new_parts = [parts] if later and step == 1 else []
                moved = tie(left, right, *received, *[found[k] for k in keys], *new_parts)
                left, right = moved[:2]
                moved = moved[2:]
                received, moved = moved[: len(received)], moved[len(received) :]
                found = dict(zip(keys, moved))
                if new_parts:
                    partial = lookup((all_offsets, moved[-1]))
                if result is not None:
                    result, left, right = tie(result, left, right)
        column.update(partner_step(groups, found))
        if later:
            received = reduce_step(partial, groups - 1, received)

    if use_kernels:
        for part in range(LAST_PARTS):
            result = multiply(groups - 1 + part / LAST_PARTS, result)
        result = result.reshape(band, -1, 2, LANES).transpose(2, 0, 1, 3)
    else:

        def in_order(own, held):
            turned = [own]
            for offset in range(1, groups):
                from_right = own_group + offset < groups
                turned.append(jnp.where(from_right, held[offset][0], held[groups - offset][1]))
            return jnp.roll(jnp.stack(turned), own_group, axis=0)

        all_rows = jnp.concatenate([in_order(*pair) for pair in rows], axis=2)
        all_columns = jnp.stack([jnp.concatenate([columns[c][k] for c in range(CHUNKS)], axis=1) for k in range(band)])
        result = jnp.einsum(
            "sfrt,kfct->fksrc", all_rows, all_columns, preferred_element_type=jnp.float32
        )
        result = (result * inverse_count).astype(jnp.bfloat16)
    return result.reshape(1, 2, band, 1, block_width * slice_width)


def solution(mesh):
    placed = (P("dp", "tensor"), P("tensor", "dp"), P("dp", "tensor"), P("dp", "tensor"))
    return jax.shard_map(
        per_device,
        mesh=mesh,
        in_specs=placed,
        out_specs=P("tensor", None, None, "dp", None),
        check_vma=False,
    )
```

```python
import functools
import jax
import jax.numpy as jnp
import numpy as np
from jax import lax
from jax.experimental import pallas as pl
from jax.experimental.pallas import tpu as pltpu
from jax.sharding import PartitionSpec as P

CHUNKS = 1
LAST_PARTS = 2
LANES = 128
CONTRACT_LAST = (((1,), (1,)), ((), ()))


def hidden_kernel(base, table_ref, weight_ref, features_ref, out_ref):
    groups, per_group, local_tokens, local_features = features_ref.shape
    for g in range(groups):
        place = table_ref[base + g]
        total = None
        for q in range(per_group):
            part = lax.dot_general(
                weight_ref[:, q * local_features : (q + 1) * local_features],
                features_ref[place, q],
                CONTRACT_LAST,
                preferred_element_type=jnp.float32,
            )
            total = part if total is None else total + part
        out_ref[0, :, g * local_tokens : (g + 1) * local_tokens] = total


def hidden_parts(weight, features, chunk_rows, table, base, count):
    groups, per_group, local_tokens, local_features = features.shape
    width = weight.shape[1]
    tokens = groups * local_tokens
    return pl.pallas_call(
        functools.partial(hidden_kernel, base + count),
        grid_spec=pltpu.PrefetchScalarGridSpec(
            num_scalar_prefetch=1,
            grid=(count,),
            in_specs=[
                pl.BlockSpec((chunk_rows, width), lambda i, table_ref: (table_ref[base + i], 0)),
                pl.BlockSpec(features.shape, lambda i, table_ref: (0, 0, 0, 0)),
            ],
            out_specs=pl.BlockSpec((1, chunk_rows, tokens), lambda i, table_ref: (i, 0, 0)),
        ),
        out_shape=jax.ShapeDtypeStruct((count, chunk_rows, tokens), jnp.float32),
        compiler_params=pltpu.CompilerParams(
            dimension_semantics=("arbitrary",), vmem_limit_bytes=56 * 2**20
        ),
        cost_estimate=pl.CostEstimate(
            flops=2 * count * chunk_rows * tokens * width,
            bytes_accessed=count * chunk_rows * (2 * width + 4 * tokens) + 2 * tokens * width,
            transcendentals=0,
        ),
    )(table, weight, features)


def factor_kernel(shape, candidates, plan, base, scale, table_ref, *refs):
    partners, chunk_total, chunk_rows, row_count = shape
    total = len(plan)
    row_refs = refs[: sum(candidates)]
    columns = refs[len(row_refs) : len(row_refs) + partners * chunk_total]
    out_ref, held, rows_held, wide_even, wide_odd, column_sems, row_sems = refs[-7:]
    wides = (wide_even, wide_odd)
    slice_width = held.shape[2]
    lane_tiles = slice_width // LANES
    stride = 2 * lane_tiles
    step = pl.program_id(0)
    current = jnp.minimum(step, total - 1)
    slot, buffer = table_ref[base + 2 * total + current], table_ref[base + 3 * total + current]
    loads = [i for i in range(total) if i == 0 or plan[i][0] != plan[i - 1][0]]
    firsts = {}
    for i, (_, k) in enumerate(plan):
        firsts.setdefault(k, i)

    def column_copy(k, chunk):
        return pltpu.make_async_copy(
            columns[k * chunk_total + chunk],
            held.at[k, :, pl.ds(chunk * chunk_rows, chunk_rows)],
            column_sems.at[k, chunk],
        )

    def row_copy(source, place):
        return pltpu.make_async_copy(source, rows_held.at[place], row_sems.at[place])

    def fetch(load):
        piece = plan[loads[load]][0]
        first = sum(candidates[:piece])
        for choice in range(candidates[piece]):

            @pl.when(table_ref[base + 4 * total + piece] == choice)
            def _():
                row_copy(row_refs[first + choice], load % 2).start()

    @pl.when(step == 0)
    def _():
        fetch(0)
        for k in sorted(firsts, key=firsts.get):
            for chunk in range(chunk_total):
                column_copy(k, chunk).start()

    for load, i in enumerate(loads):

        @pl.when(step == i)
        def _():
            row_copy(row_refs[0], load % 2).wait()
            if load + 1 < len(loads):
                fetch(load + 1)

    for k, i in firsts.items():

        @pl.when(step == i)
        def _():
            for chunk in range(chunk_total):
                column_copy(k, chunk).wait()

    def lay_out(wide):
        out_ref[0] = wide[...].astype(out_ref.dtype)

    def multiply(wide):
        for f in range(2):
            rows = rows_held[buffer, f]
            for first in range(0, lane_tiles, 2):
                count = min(2, lane_tiles - first)
                part = held[slot, f, pl.ds(first * LANES, count * LANES), :]
                product = lax.dot_general(
                    rows, part, CONTRACT_LAST, preferred_element_type=jnp.float32
                )
                product = product * scale
                for extra in range(count):
                    start = (first + extra) * 2 + f
                    wide[pl.ds(start, row_count, stride=stride), :] = product[
                        :, extra * LANES : (extra + 1) * LANES
                    ]

    for parity in range(2):

        @pl.when((step % 2 == parity) & (step < total))
        def _():
            multiply(wides[parity])
            lay_out(wides[1 - parity])

    @pl.when(step == total)
    def _():
        lay_out(wides[(total - 1) % 2])


def factor_table(plan, used, keys, positions, choices):
    buffers = [0]
    for last, now in zip(plan, plan[1:]):
        buffers.append(buffers[-1] if last[0] == now[0] else 1 - buffers[-1])
    return (
        [positions[piece] for piece, _ in plan]
        + [k for _, k in plan]
        + [keys.index(k) for _, k in plan]
        + buffers
        + [choices[piece] for piece in used]
    )


def factor_rows(pieces, columns, plan, table, base, previous, band, slices, scale):
    used, keys = sorted(pieces), sorted(columns)
    plan = [(used.index(piece), k) for piece, k in plan]
    pieces = [pieces[piece] for piece in used]
    _, row_count, tokens = pieces[0][0].shape
    dtype = pieces[0][0].dtype
    chunk_total = len(columns[keys[0]])
    chunk_rows = columns[keys[0]][0].shape[1]
    slice_width = chunk_total * chunk_rows
    lane_tiles = slice_width // LANES
    height = row_count * 2 * lane_tiles
    operands = [array for arrays in pieces for array in arrays]
    operands += [part for k in keys for part in columns[k]]
    aliases = {}
    if previous is not None:
        aliases = {1 + len(operands): 0}
        operands.append(previous)
    total = len(plan)

    def placed(step, table_ref):
        done = jnp.maximum(step - 1, 0)
        return table_ref[base + total + done], table_ref[base + done], 0

    return pl.pallas_call(
        functools.partial(
            factor_kernel,
            (len(keys), chunk_total, chunk_rows, row_count),
            tuple(len(arrays) for arrays in pieces),
            tuple((piece, keys.index(k)) for piece, k in plan),
            base,
            scale,
        ),
        grid_spec=pltpu.PrefetchScalarGridSpec(
            num_scalar_prefetch=1,
            grid=(total + 1,),
            in_specs=[pl.BlockSpec(memory_space=pl.ANY)] * len(operands),
            out_specs=pl.BlockSpec((1, height, LANES), placed),
            scratch_shapes=[
                pltpu.VMEM((len(keys), 2, slice_width, tokens), dtype),
                pltpu.VMEM((2, 2, row_count, tokens), dtype),
                pltpu.VMEM((height, LANES), jnp.float32),
                pltpu.VMEM((height, LANES), jnp.float32),
                pltpu.SemaphoreType.DMA((len(keys), chunk_total)),
                pltpu.SemaphoreType.DMA((2,)),
            ],
        ),
        out_shape=jax.ShapeDtypeStruct(
            (band, slices * slice_width * 2 * lane_tiles, LANES), dtype
        ),
        input_output_aliases=aliases,
        compiler_params=pltpu.CompilerParams(
            dimension_semantics=("arbitrary",), vmem_limit_bytes=56 * 2**20
        ),
        cost_estimate=pl.CostEstimate(
            flops=4 * total * row_count * tokens * slice_width,
            bytes_accessed=4 * total * row_count * (tokens + slice_width)
            + 4 * len(keys) * slice_width * tokens,
            transcendentals=0,
        ),
    )(table, *operands)


def tie(*arrays):
    return lax.optimization_barrier(arrays)


def arrivals(groups, d):
    found = []
    for hops in range(1, groups):
        if d + hops < groups:
            found.append((hops, False))
        if d - hops >= 0:
            found.append((hops, True))
    return found


def per_device(cotangent, down_weight, gate_pre, up_pre):
    blocks = lax.axis_size("tensor")
    groups = lax.axis_size("dp")
    own_block = lax.axis_index("tensor")
    own_group = lax.axis_index("dp")
    per_group = blocks // groups
    local_tokens, block_width = gate_pre.shape
    local_features = cotangent.shape[1]
    slice_width = block_width // groups
    all_tokens = local_tokens * groups
    half_band = blocks // 2
    chunk_rows = slice_width // CHUNKS
    use_kernels = (
        slice_width % LANES == 0
        and chunk_rows % (16 * LAST_PARTS) == 0
        and local_features % LANES == 0
        and local_tokens % LANES == 0
    )

    to_plane = [
        ((m * per_group + q) * groups + g, ((m + g) % groups * per_group + q) * groups + m)
        for m in range(groups)
        for q in range(per_group)
        for g in range(groups)
    ]
    sent = lax.ppermute(cotangent, ("tensor", "dp"), to_plane)
    saved = jnp.stack([gate_pre.T, up_pre.T])
    sent, saved = tie(sent, saved)
    features = lax.all_gather(sent, "tensor", axis=0, tiled=True)

    def saved_pieces(chunk, saved, nothing):
        def part(index):
            first = (index % groups) * slice_width + chunk * chunk_rows + nothing
            return lax.dynamic_slice_in_dim(saved, first, chunk_rows, 1)

        pieces = [part(own_group)]
        for shift in range(1, groups):
            ring = [(d, (d + shift) % groups) for d in range(groups)]
            pieces.append(lax.ppermute(part(own_group + shift), "dp", ring))
        return pieces

    def order_saved(pieces):
        pieces = jnp.stack(pieces)
        return jnp.concatenate(
            [
                lax.dynamic_index_in_dim(pieces, (own_group - h) % groups, 0, keepdims=False)
                for h in range(groups)
            ],
            axis=2,
        )

    arrived = sent[:16, :LANES]
    signs = [
        lax.ppermute(arrived, "dp", [(d, (d + shift) % groups) for d in range(groups)])
        for shift in range(1, groups)
    ]
    nothing = sum(jnp.minimum(jnp.abs(sign[0, 0].astype(jnp.float32)), 0.0) for sign in signs)
    first_saved = saved_pieces(0, saved, nothing.astype(jnp.int32))
    features = features.reshape(groups, per_group, local_tokens, local_features)

    def partial_products(chunk, offsets, features):
        count = len(offsets[0])
        if use_kernels:
            base = bases["hidden", chunk, offsets]
            return hidden_parts(down_weight, features, chunk_rows, table, base, count)
        ordered = jnp.roll(features, -own_group, axis=0)
        own_offsets = jnp.asarray(np.array(offsets, np.int32))[own_group]
        made = []
        for offset in [own_offsets[place] for place in range(count)]:
            first = (own_group + offset) % groups * slice_width + chunk * chunk_rows
            part = lax.dynamic_slice_in_dim(down_weight, first, chunk_rows, 0)
            made.append(
                jnp.einsum(
                    "uqw,gqtw->ugt",
                    part.reshape(chunk_rows, per_group, local_features),
                    ordered,
                    preferred_element_type=jnp.float32,
                ).reshape(chunk_rows, all_tokens)
            )
        return jnp.stack(made)

    def reduce_step(partial, step, received):
        if step == 1 and groups > 3:
            ends = [(0, 1), (groups - 1, groups - 2)]
            moved = lax.ppermute(partial("first").astype(jnp.bfloat16), "dp", ends)
            return moved, moved
        right, left = partial(groups - step), partial(step)
        if received is not None:
            right = right + received[0].astype(jnp.float32)
            left = left + received[1].astype(jnp.float32)
        return (
            lax.ppermute(right.astype(jnp.bfloat16), "dp", [(d, d + 1) for d in range(step)]),
            lax.ppermute(
                left.astype(jnp.bfloat16),
                "dp",
                [(d, d - 1) for d in range(groups - step, groups)],
            ),
        )

    def gradients(partial, received, saved):
        hidden_cot = partial(0) + received[0].astype(jnp.float32) + received[1].astype(jnp.float32)
        local = saved.astype(jnp.float32)
        gate_value, up_value = local[0], local[1]
        sigmoid_gate = jax.nn.sigmoid(gate_value)
        grad_gate = hidden_cot * up_value * sigmoid_gate * (1.0 + gate_value * (1.0 - sigmoid_gate))
        grad_up = hidden_cot * gate_value * sigmoid_gate
        return jnp.stack([grad_gate.astype(jnp.bfloat16), grad_up.astype(jnp.bfloat16)])

    def gather_step(step, left, right):
        return (
            lax.ppermute(left, "dp", [(d, d + 1) for d in range(step - 1, groups - 1)]),
            lax.ppermute(right, "dp", [(d, d - 1) for d in range(1, groups - step + 1)]),
        )

    shifts = list(range(2, half_band + 1, 2))
    turns = max(groups - 2, 1)
    share = -(-len(shifts) // turns)

    def partner_step(step, found):
        made = {}
        if step > 1:
            swap = [(t, t ^ 1) for t in range(blocks)]
            odd = own_block % 2 == 1
            for k in range(1, half_band, 2):
                if k not in found and k - 1 in found and k + 1 in found:
                    made[k] = lax.ppermute(
                        jnp.where(odd, found[k + 1], found[k - 1]), "tensor", swap
                    )
        for k in shifts[(step - 1) * share : step * share]:
            made[k] = lax.ppermute(
                found[0], "tensor", [(t, (t + k) % blocks) for t in range(blocks)]
            )
        return made

    band = half_band + 1
    inverse_count = 1.0 / all_tokens
    order = [arrivals(groups, d) for d in range(groups)]

    ready = {0: 0}
    for place, k in enumerate(shifts):
        ready[k] = place // share + 1
    for k in range(1, half_band, 2):
        ready[k] = max(ready[k - 1], ready[k + 1]) + 1
        if ready[k] == groups - 1:
            ready[k] -= 0.5
    calls = {}
    for k in sorted(ready, key=ready.get):
        for chunk in range(CHUNKS):
            for place in range(groups):
                came = 0
                if chunk == CHUNKS - 1 and place:
                    came = max(order[d][place - 1][0] for d in range(groups))
                if came == groups - 1:
                    for part in range(LAST_PARTS):
                        time = came + part / LAST_PARTS
                        calls.setdefault(time, []).append(((chunk, place, part), k))
                else:
                    calls.setdefault(max(ready[k], came), []).append(((chunk, place, None), k))

    part_rows = chunk_rows // LAST_PARTS

    def row_arrays(chunk, place, part):
        own, held = rows[chunk]
        if place == 0:
            return [own]
        kinds = sorted({order[d][place - 1] for d in range(groups)})
        arrays = [held[hops][int(left)] for hops, left in kinds]
        if part is None:
            return arrays
        return [
            parts[part] if hops == groups - 1 else piece_of(parts, part)
            for (hops, _), parts in zip(kinds, arrays)
        ]

    def piece_of(array, part):
        return array[:, part * part_rows : (part + 1) * part_rows]

    def row_entry(d, chunk, place, part):
        hops, left, choice = 0, False, 0
        if place:
            kinds = sorted({order[e][place - 1] for e in range(groups)})
            hops, left = order[d][place - 1]
            choice = kinds.index((hops, left))
        position = (d - hops if left else d + hops) * CHUNKS + chunk
        if part is not None:
            position = position * LAST_PARTS + part
        return position, choice

    middle = (0, *range(2, groups - 1))
    first_offsets = tuple((groups - 1,) if d == 0 else (1,) for d in range(groups))
    other_offsets = tuple(
        (*middle, 1) if d == 0 else (*middle, groups - 1) for d in range(groups)
    )
    all_offsets = tuple(
        (*first_offsets[d], *other_offsets[d]) for d in range(groups)
    )
    hidden_calls = [(0, first_offsets), (0, other_offsets)]
    hidden_calls += [(chunk, all_offsets) for chunk in range(1, CHUNKS)]
    bases, lines = {}, [[] for _ in range(groups)]
    for chunk, offsets in hidden_calls:
        bases["hidden", chunk, offsets] = len(lines[0])
        for d in range(groups):
            lines[d] += [(d + offset) % groups * CHUNKS + chunk for offset in offsets[d]]
            lines[d] += [(d + g) % groups for g in range(groups)]
    for time, plan in calls.items():
        bases["factor", time] = len(lines[0])
        used = sorted({piece for piece, _ in plan})
        keys = sorted({k for _, k in plan})
        for d in range(groups):
            entries = [row_entry(d, *piece) for piece in used]
            lines[d] += factor_table(
                [(used.index(piece), k) for piece, k in plan],
                list(range(len(used))),
                keys,
                [position for position, _ in entries],
                [choice for _, choice in entries],
            )
    table = lax.dynamic_index_in_dim(
        jnp.asarray(np.array(lines, np.int32)), own_group, 0, keepdims=False
    )

    def multiply(time, result):
        if time not in calls:
            return result
        plan = calls[time]
        pieces = {piece: row_arrays(*piece) for piece, _ in plan}
        parts = {k: [columns[c][k] for c in range(CHUNKS)] for _, k in plan}
        base = bases["factor", time]
        return factor_rows(
            pieces, parts, plan, table, base, result, band, groups, inverse_count
        )

    def lookup(first, others):
        def partial(offset):
            if offset == "first":
                return first
            if offset in middle:
                return others[middle.index(offset)]
            return jnp.where((own_group == 0) == (offset == 1), others[len(middle)], first)

        return partial

    first_parts = partial_products(0, first_offsets, features)
    first_parts, first_saved[1], first_saved[-1] = tie(
        first_parts, first_saved[1], first_saved[-1]
    )
    other_parts = partial_products(0, other_offsets, features)
    partial = lookup(first_parts[0], other_parts)
    later_saved = [saved_pieces(chunk, saved, 0) for chunk in range(1, CHUNKS)]
    received = None
    for step in range(1, groups):
        received = tie(*reduce_step(partial, step, received))
        if step == 1:
            moved = tie(*received, *first_saved)
            received, first_saved = moved[:2], list(moved[2:])
        if step == groups - 2 and later_saved:
            moved = tie(*received, *[piece for pieces in later_saved for piece in pieces])
            received, moved = moved[:2], moved[2:]
            later_saved = [
                list(moved[c * groups : (c + 1) * groups]) for c in range(CHUNKS - 1)
            ]
    all_saved = [order_saved(pieces) for pieces in [first_saved, *later_saved]]
    rows, columns, result = [], [], None
    for chunk in range(CHUNKS):
        own = gradients(partial, received, all_saved[chunk])
        own, features = tie(own, features)
        later = chunk + 1 < CHUNKS
        received = ()
        if later:
            parts = partial_products(chunk + 1, all_offsets, features)
        held, column, found = {}, {0: own}, {0: own}
        rows.append((own, held))
        columns.append(column)
        left = right = own
        for step in range(1, groups):
            if later and step > 1:
                received = reduce_step(partial, step - 1, received or None)
            made = partner_step(step, found)
            if step < groups - 1 or later or not use_kernels:
                left, right = gather_step(step, left, right)
                held[step] = (right, left)
            else:
                lefts, rights, sent_on = [], [], ()
                for part in range(LAST_PARTS):
                    ends = (piece_of(left, part), piece_of(right, part))
                    if sent_on:
                        ends = tie(*ends, *sent_on)[:2]
                    sent_on = gather_step(step, *ends)
                    lefts.append(sent_on[0])
                    rights.append(sent_on[1])
                held[step] = (rights, lefts)
            column.update(made)
            found.update(made)
            if use_kernels and not later:
                result = multiply(step - 1, result)
                result = multiply(step - 0.5, result)
            if step < groups - 1 or later:
                keys = list(found)
                new_parts = [parts] if later and step == 1 else []
                moved = tie(left, right, *received, *[found[k] for k in keys], *new_parts)
                left, right = moved[:2]
                moved = moved[2:]
                received, moved = moved[: len(received)], moved[len(received) :]
                found = dict(zip(keys, moved))
                if new_parts:
                    partial = lookup(moved[-1][0], moved[-1][1:])
                if result is not None:
                    result, left, right = tie(result, left, right)
        column.update(partner_step(groups, found))
        if later:
            received = reduce_step(partial, groups - 1, received)

    if use_kernels:
        for part in range(LAST_PARTS):
            result = multiply(groups - 1 + part / LAST_PARTS, result)
        result = result.reshape(band, -1, 2, LANES).transpose(2, 0, 1, 3)
    else:

        def in_order(own, held):
            turned = [own]
            for offset in range(1, groups):
                from_right = own_group + offset < groups
                turned.append(jnp.where(from_right, held[offset][0], held[groups - offset][1]))
            return jnp.roll(jnp.stack(turned), own_group, axis=0)

        all_rows = jnp.concatenate([in_order(*pair) for pair in rows], axis=2)
        all_columns = jnp.stack([jnp.concatenate([columns[c][k] for c in range(CHUNKS)], axis=1) for k in range(band)])
        result = jnp.einsum(
            "sfrt,kfct->fksrc", all_rows, all_columns, preferred_element_type=jnp.float32
        )
        result = (result * inverse_count).astype(jnp.bfloat16)
    return result.reshape(1, 2, band, 1, block_width * slice_width)


def solution(mesh):
    placed = (P("dp", "tensor"), P("tensor", "dp"), P("dp", "tensor"), P("dp", "tensor"))
    return jax.shard_map(
        per_device,
        mesh=mesh,
        in_specs=placed,
        out_specs=P("tensor", None, None, "dp", None),
        check_vma=False,
    )
```

```python
import functools
import jax
import jax.numpy as jnp
import numpy as np
from jax import lax
from jax.experimental import pallas as pl
from jax.experimental.pallas import tpu as pltpu
from jax.sharding import PartitionSpec as P

CHUNKS = 1
LAST_PARTS = 2
LANES = 128
CONTRACT_LAST = (((1,), (1,)), ((), ()))


def hidden_kernel(base, table_ref, weight_ref, features_ref, out_ref):
    groups, per_group, local_tokens, local_features = features_ref.shape
    for g in range(groups):
        place = table_ref[base + g]
        total = None
        for q in range(per_group):
            part = lax.dot_general(
                weight_ref[:, q * local_features : (q + 1) * local_features],
                features_ref[place, q],
                CONTRACT_LAST,
                preferred_element_type=jnp.float32,
            )
            total = part if total is None else total + part
        out_ref[0, :, g * local_tokens : (g + 1) * local_tokens] = total


def hidden_parts(weight, features, chunk_rows, table, base, count):
    groups, per_group, local_tokens, local_features = features.shape
    width = weight.shape[1]
    tokens = groups * local_tokens
    return pl.pallas_call(
        functools.partial(hidden_kernel, base + count),
        grid_spec=pltpu.PrefetchScalarGridSpec(
            num_scalar_prefetch=1,
            grid=(count,),
            in_specs=[
                pl.BlockSpec((chunk_rows, width), lambda i, table_ref: (table_ref[base + i], 0)),
                pl.BlockSpec(features.shape, lambda i, table_ref: (0, 0, 0, 0)),
            ],
            out_specs=pl.BlockSpec((1, chunk_rows, tokens), lambda i, table_ref: (i, 0, 0)),
        ),
        out_shape=jax.ShapeDtypeStruct((count, chunk_rows, tokens), jnp.float32),
        compiler_params=pltpu.CompilerParams(
            dimension_semantics=("arbitrary",), vmem_limit_bytes=56 * 2**20
        ),
        cost_estimate=pl.CostEstimate(
            flops=2 * count * chunk_rows * tokens * width,
            bytes_accessed=count * chunk_rows * (2 * width + 4 * tokens) + 2 * tokens * width,
            transcendentals=0,
        ),
    )(table, weight, features)


def factor_kernel(shape, candidates, plan, base, scale, table_ref, *refs):
    partners, chunk_total, chunk_rows, row_count = shape
    total = len(plan)
    row_refs = refs[: sum(candidates)]
    columns = refs[len(row_refs) : len(row_refs) + partners * chunk_total]
    out_ref, held, rows_held, wide_even, wide_odd, column_sems, row_sems = refs[-7:]
    wides = (wide_even, wide_odd)
    slice_width = held.shape[2]
    lane_tiles = slice_width // LANES
    stride = 2 * lane_tiles
    step = pl.program_id(0)
    current = jnp.minimum(step, total - 1)
    slot, buffer = table_ref[base + 2 * total + current], table_ref[base + 3 * total + current]
    loads = [i for i in range(total) if i == 0 or plan[i][0] != plan[i - 1][0]]
    firsts = {}
    for i, (_, k) in enumerate(plan):
        firsts.setdefault(k, i)

    def column_copy(k, chunk):
        return pltpu.make_async_copy(
            columns[k * chunk_total + chunk],
            held.at[k, :, pl.ds(chunk * chunk_rows, chunk_rows)],
            column_sems.at[k, chunk],
        )

    def row_copy(source, place):
        return pltpu.make_async_copy(source, rows_held.at[place], row_sems.at[place])

    def fetch(load):
        piece = plan[loads[load]][0]
        first = sum(candidates[:piece])
        for choice in range(candidates[piece]):

            @pl.when(table_ref[base + 4 * total + piece] == choice)
            def _():
                row_copy(row_refs[first + choice], load % 2).start()

    @pl.when(step == 0)
    def _():
        fetch(0)
        for k in sorted(firsts, key=firsts.get):
            for chunk in range(chunk_total):
                column_copy(k, chunk).start()

    for load, i in enumerate(loads):

        @pl.when(step == i)
        def _():
            row_copy(row_refs[0], load % 2).wait()
            if load + 1 < len(loads):
                fetch(load + 1)

    for k, i in firsts.items():

        @pl.when(step == i)
        def _():
            for chunk in range(chunk_total):
                column_copy(k, chunk).wait()

    def lay_out(wide):
        out_ref[0] = wide[...].astype(out_ref.dtype)

    def multiply(wide):
        for f in range(2):
            rows = rows_held[buffer, f]
            for first in range(0, lane_tiles, 2):
                count = min(2, lane_tiles - first)
                part = held[slot, f, pl.ds(first * LANES, count * LANES), :]
                product = lax.dot_general(
                    rows, part, CONTRACT_LAST, preferred_element_type=jnp.float32
                )
                product = product * scale
                for extra in range(count):
                    start = (first + extra) * 2 + f
                    wide[pl.ds(start, row_count, stride=stride), :] = product[
                        :, extra * LANES : (extra + 1) * LANES
                    ]

    for parity in range(2):

        @pl.when((step % 2 == parity) & (step < total))
        def _():
            multiply(wides[parity])
            lay_out(wides[1 - parity])

    @pl.when(step == total)
    def _():
        lay_out(wides[(total - 1) % 2])


def factor_table(plan, used, keys, positions, choices):
    buffers = [0]
    for last, now in zip(plan, plan[1:]):
        buffers.append(buffers[-1] if last[0] == now[0] else 1 - buffers[-1])
    return (
        [positions[piece] for piece, _ in plan]
        + [k for _, k in plan]
        + [keys.index(k) for _, k in plan]
        + buffers
        + [choices[piece] for piece in used]
    )


def factor_rows(pieces, columns, plan, table, base, previous, band, slices, scale):
    used, keys = sorted(pieces), sorted(columns)
    plan = [(used.index(piece), k) for piece, k in plan]
    pieces = [pieces[piece] for piece in used]
    _, row_count, tokens = pieces[0][0].shape
    dtype = pieces[0][0].dtype
    chunk_total = len(columns[keys[0]])
    chunk_rows = columns[keys[0]][0].shape[1]
    slice_width = chunk_total * chunk_rows
    lane_tiles = slice_width // LANES
    height = row_count * 2 * lane_tiles
    operands = [array for arrays in pieces for array in arrays]
    operands += [part for k in keys for part in columns[k]]
    aliases = {}
    if previous is not None:
        aliases = {1 + len(operands): 0}
        operands.append(previous)
    total = len(plan)

    def placed(step, table_ref):
        done = jnp.maximum(step - 1, 0)
        return table_ref[base + total + done], table_ref[base + done], 0

    return pl.pallas_call(
        functools.partial(
            factor_kernel,
            (len(keys), chunk_total, chunk_rows, row_count),
            tuple(len(arrays) for arrays in pieces),
            tuple((piece, keys.index(k)) for piece, k in plan),
            base,
            scale,
        ),
        grid_spec=pltpu.PrefetchScalarGridSpec(
            num_scalar_prefetch=1,
            grid=(total + 1,),
            in_specs=[pl.BlockSpec(memory_space=pl.ANY)] * len(operands),
            out_specs=pl.BlockSpec((1, height, LANES), placed),
            scratch_shapes=[
                pltpu.VMEM((len(keys), 2, slice_width, tokens), dtype),
                pltpu.VMEM((2, 2, row_count, tokens), dtype),
                pltpu.VMEM((height, LANES), jnp.float32),
                pltpu.VMEM((height, LANES), jnp.float32),
                pltpu.SemaphoreType.DMA((len(keys), chunk_total)),
                pltpu.SemaphoreType.DMA((2,)),
            ],
        ),
        out_shape=jax.ShapeDtypeStruct(
            (band, slices * slice_width * 2 * lane_tiles, LANES), dtype
        ),
        input_output_aliases=aliases,
        compiler_params=pltpu.CompilerParams(
            dimension_semantics=("arbitrary",), vmem_limit_bytes=56 * 2**20
        ),
        cost_estimate=pl.CostEstimate(
            flops=4 * total * row_count * tokens * slice_width,
            bytes_accessed=4 * total * row_count * (tokens + slice_width)
            + 4 * len(keys) * slice_width * tokens,
            transcendentals=0,
        ),
    )(table, *operands)


def tie(*arrays):
    return lax.optimization_barrier(arrays)


def arrivals(groups, d):
    found = []
    for hops in range(1, groups):
        if d + hops < groups:
            found.append((hops, False))
        if d - hops >= 0:
            found.append((hops, True))
    return found


def per_device(cotangent, down_weight, gate_pre, up_pre):
    blocks = lax.axis_size("tensor")
    groups = lax.axis_size("dp")
    own_block = lax.axis_index("tensor")
    own_group = lax.axis_index("dp")
    per_group = blocks // groups
    local_tokens, block_width = gate_pre.shape
    local_features = cotangent.shape[1]
    slice_width = block_width // groups
    all_tokens = local_tokens * groups
    half_band = blocks // 2
    chunk_rows = slice_width // CHUNKS
    use_kernels = (
        slice_width % LANES == 0
        and chunk_rows % (16 * LAST_PARTS) == 0
        and local_features % LANES == 0
        and local_tokens % LANES == 0
    )

    to_plane = [
        ((m * per_group + q) * groups + g, ((m + g) % groups * per_group + q) * groups + m)
        for m in range(groups)
        for q in range(per_group)
        for g in range(groups)
    ]
    sent = lax.ppermute(cotangent, ("tensor", "dp"), to_plane)
    saved = jnp.stack([gate_pre.T, up_pre.T])
    sent, saved = tie(sent, saved)
    features = lax.all_gather(sent, "tensor", axis=0, tiled=True)

    def saved_pieces(chunk, saved, nothing):
        def part(index):
            first = (index % groups) * slice_width + chunk * chunk_rows + nothing
            return lax.dynamic_slice_in_dim(saved, first, chunk_rows, 1)

        pieces = [part(own_group)]
        for shift in range(1, groups):
            ring = [(d, (d + shift) % groups) for d in range(groups)]
            pieces.append(lax.ppermute(part(own_group + shift), "dp", ring))
        return pieces

    def order_saved(pieces):
        pieces = jnp.stack(pieces)
        return jnp.concatenate(
            [
                lax.dynamic_index_in_dim(pieces, (own_group - h) % groups, 0, keepdims=False)
                for h in range(groups)
            ],
            axis=2,
        )

    arrived = sent[:16, :LANES]
    signs = [
        lax.ppermute(arrived, "dp", [(d, (d + shift) % groups) for d in range(groups)])
        for shift in range(1, groups)
    ]
    nothing = sum(jnp.minimum(jnp.abs(sign[0, 0].astype(jnp.float32)), 0.0) for sign in signs)
    first_saved = saved_pieces(0, saved, nothing.astype(jnp.int32))
    features = features.reshape(groups, per_group, local_tokens, local_features)

    def partial_products(chunk, offsets, features):
        count = len(offsets[0])
        if use_kernels:
            base = bases["hidden", chunk, offsets]
            return hidden_parts(down_weight, features, chunk_rows, table, base, count)
        ordered = jnp.roll(features, -own_group, axis=0)
        own_offsets = jnp.asarray(np.array(offsets, np.int32))[own_group]
        made = []
        for offset in [own_offsets[place] for place in range(count)]:
            first = (own_group + offset) % groups * slice_width + chunk * chunk_rows
            part = lax.dynamic_slice_in_dim(down_weight, first, chunk_rows, 0)
            made.append(
                jnp.einsum(
                    "uqw,gqtw->ugt",
                    part.reshape(chunk_rows, per_group, local_features),
                    ordered,
                    preferred_element_type=jnp.float32,
                ).reshape(chunk_rows, all_tokens)
            )
        return jnp.stack(made)

    def reduce_step(partial, step, received):
        if step == 1 and groups > 3:
            ends = [(0, 1), (groups - 1, groups - 2)]
            moved = lax.ppermute(partial("first").astype(jnp.bfloat16), "dp", ends)
            return moved, moved
        right, left = partial(groups - step), partial(step)
        if received is not None:
            right = right + received[0].astype(jnp.float32)
            left = left + received[1].astype(jnp.float32)
        return (
            lax.ppermute(right.astype(jnp.bfloat16), "dp", [(d, d + 1) for d in range(step)]),
            lax.ppermute(
                left.astype(jnp.bfloat16),
                "dp",
                [(d, d - 1) for d in range(groups - step, groups)],
            ),
        )

    def gradients(partial, received, saved):
        hidden_cot = partial(0) + received[0].astype(jnp.float32) + received[1].astype(jnp.float32)
        local = saved.astype(jnp.float32)
        gate_value, up_value = local[0], local[1]
        sigmoid_gate = jax.nn.sigmoid(gate_value)
        grad_gate = hidden_cot * up_value * sigmoid_gate * (1.0 + gate_value * (1.0 - sigmoid_gate))
        grad_up = hidden_cot * gate_value * sigmoid_gate
        return jnp.stack([grad_gate.astype(jnp.bfloat16), grad_up.astype(jnp.bfloat16)])

    def gather_step(step, left, right):
        return (
            lax.ppermute(left, "dp", [(d, d + 1) for d in range(step - 1, groups - 1)]),
            lax.ppermute(right, "dp", [(d, d - 1) for d in range(1, groups - step + 1)]),
        )

    shifts = list(range(2, half_band + 1, 2))
    turns = max(groups - 2, 1)
    share = -(-len(shifts) // turns)

    def partner_step(step, found):
        made = {}
        if step > 1:
            swap = [(t, t ^ 1) for t in range(blocks)]
            odd = own_block % 2 == 1
            for k in range(1, half_band, 2):
                if k not in found and k - 1 in found and k + 1 in found:
                    made[k] = lax.ppermute(
                        jnp.where(odd, found[k + 1], found[k - 1]), "tensor", swap
                    )
        for k in shifts[(step - 1) * share : step * share]:
            made[k] = lax.ppermute(
                found[0], "tensor", [(t, (t + k) % blocks) for t in range(blocks)]
            )
        return made

    band = half_band + 1
    inverse_count = 1.0 / all_tokens
    order = [arrivals(groups, d) for d in range(groups)]

    ready = {0: 0}
    for place, k in enumerate(shifts):
        ready[k] = place // share + 1
    for k in range(1, half_band, 2):
        ready[k] = max(ready[k - 1], ready[k + 1]) + 1
        if ready[k] == groups - 1:
            ready[k] -= 0.5
    calls = {}
    for k in sorted(ready, key=ready.get):
        for chunk in range(CHUNKS):
            for place in range(groups):
                came = 0
                if chunk == CHUNKS - 1 and place:
                    came = max(order[d][place - 1][0] for d in range(groups))
                if came == groups - 1:
                    for part in range(LAST_PARTS):
                        time = came + part / LAST_PARTS
                        calls.setdefault(time, []).append(((chunk, place, part), k))
                else:
                    calls.setdefault(max(ready[k], came), []).append(((chunk, place, None), k))

    part_rows = chunk_rows // LAST_PARTS

    def row_arrays(chunk, place, part):
        own, held = rows[chunk]
        if place == 0:
            return [own]
        kinds = sorted({order[d][place - 1] for d in range(groups)})
        arrays = [held[hops][int(left)] for hops, left in kinds]
        if part is None:
            return arrays
        return [
            parts[part] if hops == groups - 1 else piece_of(parts, part)
            for (hops, _), parts in zip(kinds, arrays)
        ]

    def piece_of(array, part):
        return array[:, part * part_rows : (part + 1) * part_rows]

    def row_entry(d, chunk, place, part):
        hops, left, choice = 0, False, 0
        if place:
            kinds = sorted({order[e][place - 1] for e in range(groups)})
            hops, left = order[d][place - 1]
            choice = kinds.index((hops, left))
        position = (d - hops if left else d + hops) * CHUNKS + chunk
        if part is not None:
            position = position * LAST_PARTS + part
        return position, choice

    first_offsets = tuple((groups - 1,) if d == 0 else (1,) for d in range(groups))
    other_offsets = (tuple(range(groups)),) * groups
    all_offsets = tuple((*first, *others) for first, others in zip(first_offsets, other_offsets))
    hidden_calls = [(0, first_offsets), (0, other_offsets)]
    hidden_calls += [(chunk, all_offsets) for chunk in range(1, CHUNKS)]
    bases, lines = {}, [[] for _ in range(groups)]
    for chunk, offsets in hidden_calls:
        bases["hidden", chunk, offsets] = len(lines[0])
        for d in range(groups):
            lines[d] += [(d + offset) % groups * CHUNKS + chunk for offset in offsets[d]]
            lines[d] += [(d + g) % groups for g in range(groups)]
    for time, plan in calls.items():
        bases["factor", time] = len(lines[0])
        used = sorted({piece for piece, _ in plan})
        keys = sorted({k for _, k in plan})
        for d in range(groups):
            entries = [row_entry(d, *piece) for piece in used]
            lines[d] += factor_table(
                [(used.index(piece), k) for piece, k in plan],
                list(range(len(used))),
                keys,
                [position for position, _ in entries],
                [choice for _, choice in entries],
            )
    table = lax.dynamic_index_in_dim(
        jnp.asarray(np.array(lines, np.int32)), own_group, 0, keepdims=False
    )

    def multiply(time, result):
        if time not in calls:
            return result
        plan = calls[time]
        pieces = {piece: row_arrays(*piece) for piece, _ in plan}
        parts = {k: [columns[c][k] for c in range(CHUNKS)] for _, k in plan}
        base = bases["factor", time]
        return factor_rows(
            pieces, parts, plan, table, base, result, band, groups, inverse_count
        )

    def lookup(first, others):
        def partial(offset):
            if offset == "first":
                return first
            return others[offset]

        return partial

    first_parts = partial_products(0, first_offsets, features)
    first_parts, first_saved[1], first_saved[-1] = tie(
        first_parts, first_saved[1], first_saved[-1]
    )
    other_parts = partial_products(0, other_offsets, features)
    partial = lookup(first_parts[0], other_parts)
    later_saved = [saved_pieces(chunk, saved, 0) for chunk in range(1, CHUNKS)]
    received = None
    for step in range(1, groups):
        received = tie(*reduce_step(partial, step, received))
        if step == 1:
            moved = tie(*received, *first_saved)
            received, first_saved = moved[:2], list(moved[2:])
        if step == groups - 2 and later_saved:
            moved = tie(*received, *[piece for pieces in later_saved for piece in pieces])
            received, moved = moved[:2], moved[2:]
            later_saved = [
                list(moved[c * groups : (c + 1) * groups]) for c in range(CHUNKS - 1)
            ]
    all_saved = [order_saved(pieces) for pieces in [first_saved, *later_saved]]
    rows, columns, result = [], [], None
    for chunk in range(CHUNKS):
        own = gradients(partial, received, all_saved[chunk])
        own, features = tie(own, features)
        later = chunk + 1 < CHUNKS
        received = ()
        if later:
            parts = partial_products(chunk + 1, all_offsets, features)
        held, column, found = {}, {0: own}, {0: own}
        rows.append((own, held))
        columns.append(column)
        left = right = own
        for step in range(1, groups):
            if later and step > 1:
                received = reduce_step(partial, step - 1, received or None)
            halved = use_kernels and not later and step == groups - 1
            if halved:
                keys = list(found)
                moved = tie(piece_of(left, 0), piece_of(right, 0), *found.values())
                first_ends, found = moved[:2], dict(zip(keys, moved[2:]))
            made = partner_step(step, found)
            if not halved:
                left, right = gather_step(step, left, right)
                held[step] = (right, left)
            else:
                lefts, rights, sent_on = [], [], ()
                for part in range(LAST_PARTS):
                    ends = first_ends if part == 0 else (piece_of(left, part), piece_of(right, part))
                    if sent_on:
                        ends = tie(*ends, *sent_on)[:2]
                    sent_on = gather_step(step, *ends)
                    lefts.append(sent_on[0])
                    rights.append(sent_on[1])
                held[step] = (rights, lefts)
            column.update(made)
            found.update(made)
            if use_kernels and not later:
                result = multiply(step - 1, result)
                result = multiply(step - 0.5, result)
            if step < groups - 1 or later:
                keys = list(found)
                new_parts = [parts] if later and step == 1 else []
                moved = tie(left, right, *received, *[found[k] for k in keys], *new_parts)
                left, right = moved[:2]
                moved = moved[2:]
                received, moved = moved[: len(received)], moved[len(received) :]
                found = dict(zip(keys, moved))
                if new_parts:
                    partial = lookup(moved[-1][0], moved[-1][1:])
                if result is not None:
                    result, left, right = tie(result, left, right)
        column.update(partner_step(groups, found))
        if later:
            received = reduce_step(partial, groups - 1, received)

    if use_kernels:
        for part in range(LAST_PARTS):
            result = multiply(groups - 1 + part / LAST_PARTS, result)
        result = result.reshape(band, -1, 2, LANES).transpose(2, 0, 1, 3)
    else:

        def in_order(own, held):
            turned = [own]
            for offset in range(1, groups):
                from_right = own_group + offset < groups
                turned.append(jnp.where(from_right, held[offset][0], held[groups - offset][1]))
            return jnp.roll(jnp.stack(turned), own_group, axis=0)

        all_rows = jnp.concatenate([in_order(*pair) for pair in rows], axis=2)
        all_columns = jnp.stack([jnp.concatenate([columns[c][k] for c in range(CHUNKS)], axis=1) for k in range(band)])
        result = jnp.einsum(
            "sfrt,kfct->fksrc", all_rows, all_columns, preferred_element_type=jnp.float32
        )
        result = (result * inverse_count).astype(jnp.bfloat16)
    return result.reshape(1, 2, band, 1, block_width * slice_width)


def solution(mesh):
    placed = (P("dp", "tensor"), P("tensor", "dp"), P("dp", "tensor"), P("dp", "tensor"))
    return jax.shard_map(
        per_device,
        mesh=mesh,
        in_specs=placed,
        out_specs=P("tensor", None, None, "dp", None),
        check_vma=False,
    )
```
